256 devices in a mesh: dp: 32 (over x, z), expert: 8 (over y, core).
Axes of the slice: x: 4, y: 4, z: 8, core: 2. Of those that a mesh axis runs over, the one named last changes fastest.
Arguments:
- tokens: bfloat16 [65536, 768], P(('dp', 'expert')), may hold values from -24 to 24
- expert_ids: int32 [65536, 2], P(('dp', 'expert')), may hold values from 0 to 31, all different within a row; in each aligned block of 256 rows (0 to 255, 256 to 511, ...) at most 32 rows name the same one
- gate_fixed: int32 [65536, 2], P(('dp', 'expert')), may hold values from 8192 to 65535
- cotangent: bfloat16 [65536, 768], P(('dp', 'expert')), may hold values from -24 to 24
- w_gate: bfloat16 [32, 768, 384], P('expert'), may hold values from -0.21875 to 0.21875
- w_up: bfloat16 [32, 768, 384], P('expert'), may hold values from -0.21875 to 0.21875
- w_down: bfloat16 [32, 768, 384], P('expert'), may hold values from -0.3125 to 0.3125
Outputs:
- layer_out: bfloat16 [65536, 768], P(('dp', 'expert'))
- input_grad: bfloat16 [65536, 768], P(('dp', 'expert'))
- grad_gate: float32 [32, 768, 384], P('expert', 'dp')
- grad_up: float32 [32, 768, 384], P('expert', 'dp')
- grad_down: float32 [32, 768, 384], P('expert', 'dp')
The draws below stay inside these ranges and needn't reach their ends.
Inputs may be any that keep to these rules, and one draw needn't show every extreme that they name: `expert_ids`: A row names 2 different experts. In each aligned block of 256 rows (the rows of one device) no expert is named by more than 32 rows, and in some block one expert is named by exactly 32 rows.
All inputs are finite; a program needn't handle non-finite values.
Results may differ from the reference program's by a relative error of at most 0.015.
Values may be sent and summed in bfloat16 or wider, within the bound.
No kernel may reach another device: no remote copies, remote signals or barrier semaphores. Data moves between devices by JAX's collectives and lax.ppermute only.
A program may use at most 64 MiB of HBM per device.

```python
import math
import jax
import jax.numpy as jnp
import numpy as np
from jax import lax

D = 768
FF = 384
TOP = 2
TOK_DEV = 256
EXPERTS = 32
TOKENS = 65536
CAP = 32
LOAD = 4096


def plant(result, stream_key, low, largest):
    index_at = [jax.random.randint(jax.random.fold_in(stream_key, axis), (), 0, length) for axis, length in enumerate(result.shape)]
    widest = result.shape.index(max(result.shape))
    neighbour = index_at[:widest] + [(index_at[widest] + 1) % result.shape[widest]] + index_at[widest + 1:]
    return result.at[tuple(index_at)].set(low).at[tuple(neighbour)].set(largest)


def raised(drawn, stream_key, source, target, parts, factor):
    owner, partner = [(jnp.arange(drawn.shape[dim]) // (drawn.shape[dim] // parts)).reshape([-1 if axis == dim else 1 for axis in range(drawn.ndim)]) for dim in (source, target)]
    chosen = jax.random.permutation(stream_key, parts)[partner]
    strong = (owner == chosen) | (owner == (partner + parts // 2) % parts)
    return jnp.where(strong, factor * drawn, drawn)


def shard_levels(rng, shape, split, least, top_value):
    loudness, own = 1.0, jax.random.fold_in(rng, 6)
    for dim, shards_of in split:
        steps = jnp.exp(jax.random.uniform(jax.random.fold_in(own, dim), (shards_of,), jnp.float32, least / len(split), top_value / len(split)))
        loudness = loudness * jnp.repeat(steps, shape[dim] // shards_of).reshape([-1 if axis == dim else 1 for axis in range(len(shape))])
    return loudness


def routed_block(key, own, number, rows, amount, top, most, skew):
    ranking = jax.random.permutation(key, amount)
    packed, ordinary = load_shares(amount, rows * top, most, skew, True), load_shares(amount, rows * top, most, skew, False)
    places = jnp.arange(amount)

    def named(lengths, rotation):
        used = int((lengths > 0).sum())
        fixed = max(1, used // 4)
        moved = fixed + (places - fixed + rotation * (used - fixed)) % max(1, amount - fixed)
        return jnp.zeros((amount,), jnp.int32).at[ranking[jnp.where(places < fixed, places, moved)]].set(jnp.asarray(lengths, jnp.int32))

    lengths = jnp.where(number % 4 == 0, named(packed, number // 4), named(ordinary, number - number // 4 - 1))
    mixed = jax.random.permutation(jax.random.fold_in(own, 3), amount)
    donor, receiver = mixed[0:amount // 2 * 2:2], mixed[1:amount // 2 * 2:2]
    margin = jnp.minimum(lengths[donor] - 1, most - lengths[receiver]) // 2
    margin = jnp.where((donor == ranking[0]) | (receiver == ranking[0]) | (lengths[receiver] == 0), 0, jnp.maximum(margin, 0))
    moved = jax.random.randint(jax.random.fold_in(own, 4), (amount // 2,), 0, 1 << 20) % (margin + 1)
    lengths = lengths.at[donor].add(-moved).at[receiver].add(moved)
    items = jnp.searchsorted(jnp.cumsum(lengths), jnp.arange(rows * top), side="right").astype(jnp.int32)
    table = items.reshape(top, rows).T
    table = table[jax.random.permutation(jax.random.fold_in(own, 1), rows)]
    rotation = jax.random.randint(jax.random.fold_in(own, 2), (rows, 1), 0, top)
    return jnp.take_along_axis(table, (jnp.arange(top)[None, :] + rotation) % top, axis=1)


def load_shares(count, total, most, skew, full):
    weights = [(1 << 20) // math.isqrt(standing ** skew) + 1 for standing in range(1, count + 1)]
    largest = most if full else min(most, max(-(-total // count), total * weights[0] // sum(weights)))
    least = 1 if total - largest >= count - 1 else 0
    holding, spare = [largest] + [least] * (count - 1), total - largest - least * (count - 1)
    while spare > 0:
        movable = [i for i in range(1, count) if holding[i] < largest] or [i for i in range(1, count) if holding[i] < most]
        whole, budget = sum([weights[i] for i in movable]), spare
        for i in movable:
            more = min(most - holding[i], max(1, budget * weights[i] // whole), spare)
            holding[i] = holding[i] + more
            spare = spare - more
    return np.array(holding)


def bell_draw(rng, shape, width, most, pieces=(), kind=jnp.bfloat16):
    gain = shard_levels(rng, shape, pieces, -0.22, 0.18) if pieces else 1.0
    drawn = jax.random.normal(rng, shape, jnp.float32) * width * gain
    return jnp.minimum(jnp.maximum(drawn, -most), most).astype(kind)


def noise_with(rng, dims, scale, bound, pieces, heavy, kind=jnp.bfloat16):
    values = scale * jax.random.normal(rng, dims, jnp.float32)
    if pieces:
        values = values * shard_levels(rng, dims, pieces, -0.22, 0.18)
    return jnp.clip(raised(values, jax.random.fold_in(rng, 3), *heavy), -bound, bound).astype(kind)


def setup_inputs(seed: int = 0) -> dict:
    key_list = jax.random.split(jax.random.key(seed), 8)
    tokens = noise_with(key_list[0], (TOKENS, D), 1.0, 24.0, ((0, 256),), (0, 1, 256, 6.0))
    expert_ids_keys = jax.random.split(jax.random.fold_in(key_list[1], 1), TOKENS // TOK_DEV)
    expert_ids_turns = jax.random.permutation(jax.random.fold_in(key_list[1], 3), TOKENS // TOK_DEV)
    expert_ids = jax.vmap(lambda own, number: routed_block(jax.random.fold_in(key_list[1], 2), own, number, TOK_DEV, EXPERTS, TOP, CAP, 1))(expert_ids_keys, expert_ids_turns).reshape((TOKENS, TOP))
    gate_fixed = plant(jax.random.randint(key_list[2], (TOKENS, TOP), 8192, 65536), jax.random.fold_in(key_list[2], 1), 8192, 65535).astype(jnp.int32)
    cotangent = noise_with(key_list[3], (TOKENS, D), 1.0, 24.0, ((0, 256),), (0, 1, 256, 6.0))
    w_gate = bell_draw(key_list[4], (EXPERTS, D, FF), D ** -0.5, 0.21875, ((0, 8),))
    w_up = bell_draw(key_list[5], (EXPERTS, D, FF), D ** -0.5, 0.21875, ((0, 8),))
    w_down = bell_draw(key_list[6], (EXPERTS, D, FF), FF ** -0.5, 0.3125, ((0, 8),))
    return {"tokens": tokens, "expert_ids": expert_ids, "gate_fixed": gate_fixed, "cotangent": cotangent, "w_gate": w_gate, "w_up": w_up, "w_down": w_down}


def matmul(left, right):
    return jnp.dot(left.astype(jnp.float32), right.astype(jnp.float32), precision=lax.Precision.HIGHEST)

def reference(tokens, expert_ids, gate_fixed, cotangent, w_gate, w_up, w_down):
    entries = TOKENS * TOP
    flat_ids = expert_ids.reshape(-1).astype(jnp.int32)
    blocks = flat_ids.reshape(-1, TOK_DEV * TOP)
    onehot = (blocks[:, :, None] == jnp.arange(EXPERTS, dtype=jnp.int32)[None, None, :]).astype(jnp.int32)
    slot_rank = lax.optimization_barrier(jnp.sum((jnp.cumsum(onehot, axis=1) - 1) * onehot, axis=2)).reshape(-1)
    block_of = jnp.arange(entries, dtype=jnp.int32) // (TOK_DEV * TOP)
    position = (block_of * CAP + slot_rank).astype(jnp.int32)
    rows_all = TOKENS // TOK_DEV * CAP
    slot_table = jnp.full((EXPERTS, rows_all), entries, jnp.int32)
    slot_table = slot_table.at[flat_ids, position].set(jnp.arange(entries, dtype=jnp.int32))
    gate_values = jnp.concatenate([gate_fixed.reshape(-1).astype(jnp.float32) / 65536.0, jnp.zeros((1,), jnp.float32)])
    grad_scale = 1.0 / math.sqrt(LOAD)

    def one_expert(totals, inputs):
        out_sum, grad_sum = totals
        rows, gate_w, up_w, down_w = inputs
        is_valid = rows < entries
        token_of = jnp.where(is_valid, rows // TOP, 0).astype(jnp.int32)
        rows_in = jnp.where(is_valid[:, None], tokens[token_of], jnp.zeros((), tokens.dtype))
        slot_gate = gate_values[rows]
        grads_in = (slot_gate[:, None] * cotangent[token_of].astype(jnp.float32)).astype(jnp.bfloat16)
        pre_gate = matmul(rows_in, gate_w)
        pre_up = matmul(rows_in, up_w)
        sigmoid_gate = jax.nn.sigmoid(pre_gate)
        activated = pre_gate * sigmoid_gate
        hidden = (activated * pre_up).astype(jnp.bfloat16)
        outputs = matmul(hidden, down_w.T).astype(jnp.bfloat16)
        hidden_grad = matmul(grads_in, down_w)
        gate_grad = (hidden_grad * pre_up * sigmoid_gate * (1.0 + pre_gate * (1.0 - sigmoid_gate))).astype(jnp.bfloat16)
        up_grad = (hidden_grad * activated).astype(jnp.bfloat16)
        entry_grad = (matmul(gate_grad, gate_w.T) + matmul(up_grad, up_w.T)).astype(jnp.bfloat16)
        out_sum = out_sum.at[token_of].add(slot_gate[:, None] * outputs.astype(jnp.float32))
        grad_sum = grad_sum.at[token_of].add(jnp.where(is_valid[:, None], entry_grad.astype(jnp.float32), jnp.zeros((), jnp.float32)))
        weight_gate = matmul(rows_in.T, gate_grad) * grad_scale
        weight_up = matmul(rows_in.T, up_grad) * grad_scale
        weight_down = matmul(grads_in.T, hidden) * grad_scale
        return ((out_sum, grad_sum), (weight_gate, weight_up, weight_down))
    start = (jnp.zeros((TOKENS, D), jnp.float32), jnp.zeros((TOKENS, D), jnp.float32))
    (out_sum, grad_sum), (grad_gate, grad_up, grad_down) = lax.scan(one_expert, start, (slot_table, w_gate, w_up, w_down))
    return (out_sum.astype(jnp.bfloat16), grad_sum.astype(jnp.bfloat16), grad_gate, grad_up, grad_down)
```

```python
import functools

import jax
import jax.numpy as jnp
from jax import lax
from jax.experimental import pallas as pl
from jax.experimental.pallas import tpu as pltpu
from jax.sharding import PartitionSpec as P

F32, BF16 = jnp.float32, jnp.bfloat16
META = 16


def dot(a, b, dims=((1,), (0,))):
    return lax.dot_general(a, b, (dims, ((), ())), preferred_element_type=F32)


def less_than(size, transposed):
    rows = lax.broadcasted_iota(jnp.int32, (size, size), 0)
    cols = lax.broadcasted_iota(jnp.int32, (size, size), 1)
    return ((cols < rows) if transposed else (rows < cols)).astype(F32).astype(BF16)


def expert_kernel(cap, scale, me_ref, *refs):
    tok, cot = refs[:8], refs[8:16]
    wg_ref, wu_ref, wd_ref = refs[16:19]
    ret, ga_ref, gb_ref, rows_s, grads_s = refs[19:27], *refs[27:31]
    step = pl.program_id(0)
    n_e = rows_s.shape[0]
    n_t = cot[0].shape[0]

    @pl.when(step == 0)
    def _():
        eid = (me_ref[0] * n_e + lax.broadcasted_iota(jnp.int32, (n_e, n_t), 0)).astype(F32)
        masks, gates = [], []
        for r in range(8):
            meta = tok[r][n_t : n_t + META, :n_t].astype(F32)
            row = lambda i: jnp.broadcast_to(meta[i : i + 1], (n_e, n_t))
            first, second = row(0) == eid, row(1) == eid
            g0 = (row(2) * 256.0 + row(3)) / 65536.0
            g1 = (row(4) * 256.0 + row(5)) / 65536.0
            masks.append(jnp.where(first | second, 1.0, 0.0))
            gates.append(jnp.where(first, g0, jnp.where(second, g1, 0.0)))
        mask = jnp.concatenate(masks, 0)
        rank = jnp.where(mask > 0.5, dot(mask.astype(BF16), less_than(n_t, False)), -1.0)
        slot = lax.broadcasted_iota(jnp.int32, (cap, n_t), 0).astype(F32)
        for r in range(8):
            hots, slot_gates = [], []
            for e in range(n_e):
                i = r * n_e + e
                hot = jnp.where(jnp.broadcast_to(rank[i : i + 1], (cap, n_t)) == slot, 1.0, 0.0)
                hots.append(hot)
                slot_gates.append(jnp.sum(hot * gates[r][e : e + 1], axis=1, keepdims=True))
            hot = jnp.concatenate(hots, 0).astype(BF16)
            slot_gate = jnp.concatenate(slot_gates, 0)
            rows = dot(hot, tok[r][:n_t, :]).astype(BF16)
            grads = (slot_gate * dot(hot, cot[r][...])).astype(BF16)
            for e in range(n_e):
                rows_s[e, r * cap : (r + 1) * cap, :] = rows[e * cap : (e + 1) * cap]
                grads_s[e, r * cap : (r + 1) * cap, :] = grads[e * cap : (e + 1) * cap]

    x, dy = rows_s[step], grads_s[step]
    wg, wu, wd = wg_ref[0], wu_ref[0], wd_ref[0]
    pre_gate, pre_up = dot(x, wg), dot(x, wu)
    sig = jax.nn.sigmoid(pre_gate)
    act = pre_gate * sig
    hidden = (act * pre_up).astype(BF16)
    hidden_grad = dot(dy, wd)
    gate_grad = (hidden_grad * pre_up * sig * (1.0 + pre_gate * (1.0 - sig))).astype(BF16)
    up_grad = (hidden_grad * act).astype(BF16)
    out = dot(hidden, wd, ((1,), (1,))).astype(BF16)
    entry = (dot(gate_grad, wg, ((1,), (1,))) + dot(up_grad, wu, ((1,), (1,)))).astype(BF16)
    for r in range(8):
        ret[r][0, 0] = out[r * cap : (r + 1) * cap]
        ret[r][1, 0] = entry[r * cap : (r + 1) * cap]
    ff = wg.shape[1]

    def weights(g_ref):
        g_ref[:, :ff] = (dot(x, gate_grad, ((0,), (0,))) * scale).astype(BF16)
        g_ref[:, ff : 2 * ff] = (dot(x, up_grad, ((0,), (0,))) * scale).astype(BF16)
        g_ref[:, 2 * ff :] = (dot(dy, hidden, ((0,), (0,))) * scale).astype(BF16)

    pl.when(step < n_e // 2)(lambda: weights(ga_ref))
    pl.when(step >= n_e // 2)(lambda: weights(gb_ref))


def experts(me, tok, cot, w_gate, w_up, w_down, cap, scale):
    n_e, d, ff = w_gate.shape
    n_t = cot[0].shape[0]
    whole = lambda a: pl.BlockSpec(a.shape, lambda e: (0,) * a.ndim)
    weight = pl.BlockSpec((1, d, ff), lambda e: (e, 0, 0))
    half = n_e // 2
    ret = jax.ShapeDtypeStruct((2, n_e, cap, d), BF16)
    grad = jax.ShapeDtypeStruct((d, half * 3 * ff), BF16)
    slots = 8 * cap
    return pl.pallas_call(
        functools.partial(expert_kernel, cap, scale),
        grid=(n_e,),
        in_specs=[pl.BlockSpec(memory_space=pltpu.SMEM)] + [whole(a) for a in (*tok, *cot)] + [weight] * 3,
        out_specs=[pl.BlockSpec((2, 1, cap, d), lambda e: (0, e, 0, 0))] * 8
        + [
            pl.BlockSpec((d, 3 * ff), lambda e: (0, jnp.minimum(e, half - 1))),
            pl.BlockSpec((d, 3 * ff), lambda e: (0, jnp.maximum(e - half, 0))),
        ],
        out_shape=[ret] * 8 + [grad] * 2,
        scratch_shapes=[pltpu.VMEM((n_e, slots, d), BF16), pltpu.VMEM((n_e, slots, d), BF16)],
        compiler_params=pltpu.CompilerParams(vmem_limit_bytes=48 * 2**20),
        cost_estimate=pl.CostEstimate(
            flops=18 * n_e * slots * d * ff + 4 * n_e * slots * n_t * d,
            bytes_accessed=2 * (6 * n_e * d * ff + 32 * n_t * d),
            transcendentals=n_e * slots * ff,
        ),
    )(me, *tok, *cot, w_gate, w_up, w_down)


def combine_kernel(cap, n_e, q_ref, ids_ref, gate_ref, *refs):
    ret, out_ref, grad_ref = refs[:8], refs[8], refs[9]
    n_t = ids_ref.shape[0]
    lane = lax.broadcasted_iota(jnp.int32, (n_t, 8 * n_e), 1)
    eid = jnp.zeros((n_t, 8 * n_e), jnp.int32)
    for r in range(8):
        eid = jnp.where(lane // n_e == r, q_ref[r] * n_e + lane % n_e, eid)
    first, second = ids_ref[:, 0:1] == eid, ids_ref[:, 1:2] == eid
    mask = jnp.where(first | second, 1.0, 0.0).astype(BF16)
    rank = dot(less_than(n_t, True), mask)
    rows = lax.broadcasted_iota(jnp.int32, (8 * n_e, 8 * n_e * cap), 0)
    cols = lax.broadcasted_iota(jnp.int32, (8 * n_e, 8 * n_e * cap), 1)
    spread = jnp.where(cols // cap == rows, 1.0, 0.0).astype(BF16)
    slot = (lax.broadcasted_iota(jnp.int32, (n_t, 8 * n_e * cap), 1) % cap).astype(F32)
    hots = [
        jnp.where(dot(jnp.where(m, rank, -1.0).astype(BF16), spread) == slot, 1.0, 0.0)
        for m in (first, second)
    ]
    both = (hots[0] + hots[1]).astype(BF16)
    hots = [h.astype(BF16) for h in hots]
    outs = jnp.concatenate([r[0] for r in ret], 0)
    grads = jnp.concatenate([r[1] for r in ret], 0)
    gate = gate_ref[...].astype(F32) / 65536.0
    total = gate[:, 0:1] * dot(hots[0], outs) + gate[:, 1:2] * dot(hots[1], outs)
    out_ref[...] = total.astype(BF16)
    grad_ref[...] = dot(both, grads).astype(BF16)


def combine(q, ids, gate, ret, cap, n_e):
    n_t, d = ids.shape[0], ret[0].shape[-1]
    row = jax.ShapeDtypeStruct((n_t, d), BF16)
    return pl.pallas_call(
        functools.partial(combine_kernel, cap, n_e),
        in_specs=[pl.BlockSpec(memory_space=pltpu.SMEM)] + [pl.BlockSpec(memory_space=pltpu.VMEM)] * 10,
        out_specs=[pl.BlockSpec(memory_space=pltpu.VMEM)] * 2,
        out_shape=[row, row],
        compiler_params=pltpu.CompilerParams(vmem_limit_bytes=40 * 2**20),
        cost_estimate=pl.CostEstimate(
            flops=6 * n_t * d * 8 * n_e * cap, bytes_accessed=40 * n_t * d, transcendentals=0
        ),
    )(q, ids, gate, *ret)


def ring_scatter(parts, place, n, shift):
    far, half = n // 2, parts.shape[2] // 2
    pick = lambda t: lax.dynamic_index_in_dim(parts, lax.rem(t + n, n), 0, keepdims=False)
    add = lambda a, b: (a.astype(F32) + b.astype(F32)).astype(BF16)
    block = pick(place + far)
    right, left = shift(block[:, :half], 1), shift(block[:, half:], -1)
    for away in range(far - 1, 0, -1):
        own_r, own_l = pick(place + away), pick(place - away)
        if away == far - 1:
            right = jnp.concatenate([add(own_r[:, :half], right), own_r[:, half:]], 1)
            left = jnp.concatenate([own_l[:, :half], add(own_l[:, half:], left)], 1)
        else:
            right, left = add(own_r, right), add(own_l, left)
        right, left = shift(right, 1), shift(left, -1)
    return pick(place).astype(F32) + right.astype(F32) + left.astype(F32)


def shards(nx, nz, tokens, expert_ids, gate_fixed, cotangent, w_gate, w_up, w_down):
    n_t, top = expert_ids.shape
    n_e, d, ff = w_gate.shape
    peers = lax.axis_size("expert")
    ny = peers // 2
    replicas = nx * nz
    cap = n_t * top * 2 // (n_e * peers)
    scale = float(n_t * replicas * top // n_e) ** (-0.5)
    me = lax.axis_index("expert")
    place = lax.axis_index("dp")

    def to(a, dy, dc):
        perm = [(y * 2 + c, ((y + dy) % ny) * 2 + (c ^ dc)) for y in range(ny) for c in range(2)]
        return lax.ppermute(a, "expert", perm)

    ids_t, gate_t = expert_ids.T, gate_fixed.T
    meta = jnp.stack(
        [ids_t[0], ids_t[1], gate_t[0] // 256, gate_t[0] % 256, gate_t[1] // 256, gate_t[1] % 256]
    ).astype(F32)
    meta = jnp.pad(meta, ((0, META - 6), (0, d - n_t))).astype(BF16)
    tok = {(0, 0): jnp.concatenate([tokens, meta], 0)}
    cot = {(0, 0): cotangent}
    tok[3, 0], cot[1, 0] = to(tok[0, 0], 1, 0), to(cot[0, 0], -1, 0)
    cot[3, 0], tok[1, 0] = to(cot[0, 0], 1, 0), to(tok[0, 0], -1, 0)
    tok[2, 0], cot[2, 0] = to(tok[3, 0], 1, 0), to(cot[1, 0], -1, 0)
    for dy in range(4):
        tok[dy, 1], cot[dy, 1] = to(tok[dy, 0], 0, 1), to(cot[dy, 0], 0, 1)
    order = [(dy, dc) for dy in range(4) for dc in range(2)]
    *ret, grads_a, grads_b = experts(
        me.reshape(1), [tok[r] for r in order], [cot[r] for r in order], w_gate, w_up, w_down, cap, scale
    )

    def x_shift(a, by):
        return lax.ppermute(
            a, "dp", [(x * nz + z, ((x + by) % nx) * nz + z) for x in range(nx) for z in range(nz)]
        )

    def z_shift(a, by):
        return lax.ppermute(
            a, "dp", [(x * nz + z, x * nz + (z + by) % nz) for x in range(nx) for z in range(nz)]
        )

    at_x, at_z = place // nz, place % nz
    wide = n_e // 2 * 3 * ff
    own = d // replicas
    a = ring_scatter(grads_a.reshape(nx, nz * own, wide), at_x, nx, x_shift).astype(BF16)
    b = grads_b.reshape(nx, nz, own, wide).swapaxes(0, 1).reshape(nz, nx * own, wide)
    b = ring_scatter(b, at_z, nz, z_shift).astype(BF16)
    a = ring_scatter(a.reshape(nz, own, wide), at_z, nz, z_shift)
    b = ring_scatter(b.reshape(nx, own, wide), at_x, nx, x_shift)
    back = [ret[0]] + [to(ret[i], *order[i]) for i in range(1, 8)]
    y, c = me // 2, me % 2
    q = jnp.stack([((y - dy + ny) % ny) * 2 + (c + dc) % 2 for dy, dc in order])
    layer_out, input_grad = combine(
        q, expert_ids, gate_fixed, [b.reshape(2, n_e * cap, d) for b in back], cap, n_e
    )
    total = jnp.concatenate([a.reshape(own, n_e // 2, 3, ff), b.reshape(own, n_e // 2, 3, ff)], 1)
    total = total.transpose(2, 1, 0, 3)
    return (layer_out, input_grad, total[0], total[1], total[2])


def solution(mesh):
    nx = 4
    nz = mesh.shape["dp"] // nx
    return jax.shard_map(
        functools.partial(shards, nx, nz),
        mesh=mesh,
        in_specs=(P(("dp", "expert"), None),) * 4 + (P("expert", None, None),) * 3,
        out_specs=(P(("dp", "expert"), None),) * 2 + (P("expert", "dp", None),) * 3,
        check_vma=False,
    )
```

```python
import functools

import jax
import jax.numpy as jnp
import numpy as np
from jax import lax
from jax.experimental import pallas as pl
from jax.experimental.pallas import tpu as pltpu
from jax.sharding import PartitionSpec as P

F32, BF16 = jnp.float32, jnp.bfloat16
META = 16


def dot(a, b, dims=((1,), (0,))):
    return lax.dot_general(a, b, (dims, ((), ())), preferred_element_type=F32)


ROOM = pltpu.CompilerParams(vmem_limit_bytes=56 * 2**20)
SCALARS = pl.BlockSpec(memory_space=pltpu.SMEM)


def whole(shape):
    return pl.BlockSpec(shape, lambda i: (0,) * len(shape))


def less_than(size, transposed):
    rows = lax.broadcasted_iota(jnp.int32, (size, size), 0)
    cols = lax.broadcasted_iota(jnp.int32, (size, size), 1)
    return ((cols < rows) if transposed else (rows < cols)).astype(F32).astype(BF16)


def meta_kernel(ids_ref, gate_ref, tok_ref, out_ref):
    n_t, d = tok_ref.shape
    ids, gate = ids_ref[...], gate_ref[...]
    high, low = gate // 256, gate % 256
    meta = jnp.concatenate([ids, high, low], 0).astype(F32)
    meta = jnp.concatenate([meta, jnp.zeros((META - 6, n_t), F32)], 0)
    out_ref[:n_t, :] = tok_ref[...]
    out_ref[n_t:, :n_t] = meta.astype(BF16)
    out_ref[n_t:, n_t:] = jnp.zeros((META, d - n_t), BF16)


def with_meta(ids, gate, tokens):
    n_t, d = tokens.shape
    return pl.pallas_call(
        meta_kernel,
        grid=(1,),
        in_specs=[whole(ids.shape), whole(gate.shape), whole(tokens.shape)],
        out_specs=whole((n_t + META, d)),
        out_shape=jax.ShapeDtypeStruct((n_t + META, d), BF16),
        compiler_params=ROOM,
        cost_estimate=pl.CostEstimate(flops=n_t * d, bytes_accessed=4 * n_t * d, transcendentals=0),
    )(ids, gate, tokens)


def pack_kernel(n, cap, n_e, me_ref, *refs):
    tok, cot = refs[:n], refs[n : 2 * n]
    rows_ref, grads_ref = refs[2 * n :]
    n_t = cot[0].shape[0]
    eid = (me_ref[0] * n_e + lax.broadcasted_iota(jnp.int32, (n_e, n_t), 0)).astype(F32)
    masks, gates = [], []
    for r in range(n):
        meta = tok[r][n_t : n_t + META, :n_t].astype(F32)
        row = lambda i: jnp.broadcast_to(meta[i : i + 1], (n_e, n_t))
        first, second = row(0) == eid, row(1) == eid
        g0 = (row(2) * 256.0 + row(4)) / 65536.0
        g1 = (row(3) * 256.0 + row(5)) / 65536.0
        masks.append(jnp.where(first | second, 1.0, 0.0))
        gates.append(jnp.where(first, g0, jnp.where(second, g1, 0.0)))
    mask = jnp.concatenate(masks, 0)
    rank = jnp.where(mask > 0.5, dot(mask.astype(BF16), less_than(n_t, False)), -1.0)
    slot = lax.broadcasted_iota(jnp.int32, (cap, n_t), 0).astype(F32)
    for r in range(n):
        hots, slot_gates = [], []
        for e in range(n_e):
            i = r * n_e + e
            hot = jnp.where(jnp.broadcast_to(rank[i : i + 1], (cap, n_t)) == slot, 1.0, 0.0)
            hots.append(hot)
            slot_gates.append(jnp.sum(hot * gates[r][e : e + 1], axis=1, keepdims=True))
        hot = jnp.concatenate(hots, 0).astype(BF16)
        slot_gate = jnp.concatenate(slot_gates, 0)
        rows = dot(hot, tok[r][:n_t, :]).astype(BF16)
        grads = (slot_gate * dot(hot, cot[r][...])).astype(BF16)
        for e in range(n_e):
            rows_ref[e, r * cap : (r + 1) * cap, :] = rows[e * cap : (e + 1) * cap]
            grads_ref[e, r * cap : (r + 1) * cap, :] = grads[e * cap : (e + 1) * cap]


def pack(me, tok, cot, cap, n_e):
    n, (n_t, d) = len(cot), cot[0].shape
    out = jax.ShapeDtypeStruct((n_e, n * cap, d), BF16)
    return pl.pallas_call(
        functools.partial(pack_kernel, n, cap, n_e),
        grid=(1,),
        in_specs=[SCALARS] + [whole(a.shape) for a in (*tok, *cot)],
        out_specs=[whole(out.shape)] * 2,
        out_shape=[out, out],
        compiler_params=ROOM,
        cost_estimate=pl.CostEstimate(
            flops=4 * n * n_e * cap * n_t * d, bytes_accessed=4 * n * (n_t + n_e * cap) * d, transcendentals=0
        ),
    )(me, *tok, *cot)


def expert_kernel(first, cap, scale, order_ref, from_ref, near_x, far_x, near_g, far_g, wg_ref, wu_ref, wd_ref, *refs):
    refs = refs[-8:]
    ret, send, keep, acc = refs[0], refs[1:3], refs[3:5], refs[5:8]
    step = pl.program_id(0)
    x = jnp.concatenate([near_x[0], far_x[0]], 0)
    dy = jnp.concatenate([near_g[0], far_g[0]], 0)
    wg, wu, wd = wg_ref[0], wu_ref[0], wd_ref[0]
    pre_gate, pre_up = dot(x, wg), dot(x, wu)
    sig = jax.nn.sigmoid(pre_gate)
    act = pre_gate * sig
    hidden = (act * pre_up).astype(BF16)
    hidden_grad = dot(dy, wd)
    gate_grad = (hidden_grad * pre_up * sig * (1.0 + pre_gate * (1.0 - sig))).astype(BF16)
    up_grad = (hidden_grad * act).astype(BF16)
    shape = acc[0].shape
    acc[0][...] = (dot(x, gate_grad, ((0,), (0,))) * scale).reshape(shape)
    acc[1][...] = (dot(x, up_grad, ((0,), (0,))) * scale).reshape(shape)
    acc[2][...] = (dot(dy, hidden, ((0,), (0,))) * scale).reshape(shape)
    out = dot(hidden, wd, ((1,), (1,))).astype(BF16)
    entry = (dot(gate_grad, wg, ((1,), (1,))) + dot(up_grad, wu, ((1,), (1,)))).astype(BF16)
    for r in range(8):
        ret[from_ref[r], 0, 0] = out[r * cap : (r + 1) * cap]
        ret[from_ref[r], 1, 0] = entry[r * cap : (r + 1) * cap]
    ff, half = wg.shape[1], shape[0] // 2
    for i in range(2):

        @pl.when(step == i)
        def _(i=i):
            for p in range(2 * half):
                chunk = order_ref[first + i, p]
                to = (send if p < half else keep)[i]
                for k in range(3):
                    to[p % half, :, k * ff : (k + 1) * ff] = acc[k][chunk].astype(BF16)


def experts(first, order, sources, near, far, weights, ret, cap, scale, replicas):
    n_e, d, ff = weights[0].shape
    slots = 8 * cap
    part = lambda a: pl.BlockSpec((1, *a.shape[1:]), lambda e: (first + e, 0, 0))
    row = pl.BlockSpec((8, 2, 1, cap, d), lambda e: (0, 0, first + e, 0, 0))
    rows = [near[0], far[0], near[1], far[1]]
    chunks = jax.ShapeDtypeStruct((replicas // 2, d // replicas, 3 * ff), BF16)
    out = pl.pallas_call(
        functools.partial(expert_kernel, first, cap, scale),
        grid=(2,),
        in_specs=[SCALARS] * 2
        + [part(a) for a in (*rows, *weights)]
        + [pl.BlockSpec(memory_space=pl.ANY)] * len(ret),
        out_specs=[row] + [whole(chunks.shape)] * 4,
        out_shape=[jax.ShapeDtypeStruct((8, 2, n_e, cap, d), BF16)] + [chunks] * 4,
        input_output_aliases={9: 0} if ret else {},
        scratch_shapes=[pltpu.VMEM((replicas, d // replicas, ff), F32)] * 3,
        compiler_params=ROOM,
        cost_estimate=pl.CostEstimate(
            flops=36 * slots * d * ff, bytes_accessed=24 * d * ff + 16 * slots * d, transcendentals=2 * slots * ff
        ),
    )(order, sources, *rows, *weights, *ret)
    return out[:1], out[1:3], out[3:5]


def combine_kernel(cap, ids_ref, gate_ref, _, ret, out_ref, grad_ref):
    n_t, count = ids_ref.shape[0], ret.shape[0] * ret.shape[2]
    eid = lax.broadcasted_iota(jnp.int32, (n_t, count), 1)
    first, second = ids_ref[:, 0:1] == eid, ids_ref[:, 1:2] == eid
    mask = jnp.where(first | second, 1.0, 0.0).astype(BF16)
    rank = dot(less_than(n_t, True), mask)
    rows = lax.broadcasted_iota(jnp.int32, (count, count * cap), 0)
    cols = lax.broadcasted_iota(jnp.int32, (count, count * cap), 1)
    spread = jnp.where(cols // cap == rows, 1.0, 0.0).astype(BF16)
    slot = (lax.broadcasted_iota(jnp.int32, (n_t, count * cap), 1) % cap).astype(F32)
    hots = [
        jnp.where(dot(jnp.where(m, rank, -1.0).astype(BF16), spread) == slot, 1.0, 0.0)
        for m in (first, second)
    ]
    both = (hots[0] + hots[1]).astype(BF16)
    hots = [h.astype(BF16) for h in hots]
    outs = ret[:, 0].reshape(count * cap, ret.shape[-1])
    grads = ret[:, 1].reshape(count * cap, ret.shape[-1])
    gate = gate_ref[...].astype(F32) / 65536.0
    total = gate[:, 0:1] * dot(hots[0], outs) + gate[:, 1:2] * dot(hots[1], outs)
    out_ref[...] = total.astype(BF16)
    grad_ref[...] = dot(both, grads).astype(BF16)


def combine(ids, gate, after, ret):
    peers, _, n_e, cap, d = ret.shape
    n_t = ids.shape[0]
    row = jax.ShapeDtypeStruct((n_t, d), BF16)
    return pl.pallas_call(
        functools.partial(combine_kernel, cap),
        grid=(1,),
        in_specs=[whole(ids.shape), whole(gate.shape), pl.BlockSpec(memory_space=pl.ANY), whole(ret.shape)],
        out_specs=[whole(row.shape)] * 2,
        out_shape=[row, row],
        compiler_params=ROOM,
        cost_estimate=pl.CostEstimate(
            flops=6 * n_t * d * peers * n_e * cap, bytes_accessed=40 * n_t * d, transcendentals=0
        ),
    )(ids, gate, after, ret)


PLANS = (
    ("xp", "xq", "zp", "zq", "zf"),
    ("xq", "xp", "zq", "zp", "zg"),
    ("zp", "zq", "xp", "xq", "zf"),
    ("zq", "zp", "xq", "xp", "zg"),
)
FAR = {"zf": (3, 6, 5, 0, 7, 2, 1, 4), "zg": (5, 4, 7, 6, 1, 0, 3, 2)}


def partners(kind, nx, nz):
    out = []
    for x in range(nx):
        for z in range(nz):
            at, n = (x, nx) if kind[0] == "x" else (z, nz)
            if kind in FAR:
                at = FAR[kind][at]
            elif kind[1] == "p":
                at = at ^ 1
            else:
                at = (at + 1) % n if at % 2 else (at - 1) % n
            out.append(at * nz + z if kind[0] == "x" else x * nz + at)
    return out


def chunk_orders(nx, nz):
    plans = []
    for plan in PLANS:
        held = [[i] for i in range(nx * nz)]
        for kind in reversed(plan):
            with_ = partners(kind, nx, nz)
            held = [held[with_[i]] + held[i] for i in range(nx * nz)]
        plans.append(held)
    return np.asarray(plans, np.int32).swapaxes(0, 1)


def reduce_grads(send, keep, nx, nz):
    send, keep = list(send), list(keep)
    swap = lambda a, kind: lax.ppermute(a, "dp", list(enumerate(partners(kind, nx, nz))))
    steps = len(PLANS[0])
    for k in range(steps):
        got = [swap(send[v], PLANS[v][k]) for v in range(4)]
        if k == steps - 1:
            return [keep[v].astype(F32) + got[v].astype(F32) for v in range(4)], send
        half = keep[0].shape[0] // 2
        for v in range(4):
            send[v] = (keep[v][:half].astype(F32) + got[v][:half].astype(F32)).astype(BF16)
            keep[v] = (keep[v][half:].astype(F32) + got[v][half:].astype(F32)).astype(BF16)


def shards(nx, nz, tokens, expert_ids, gate_fixed, cotangent, w_gate, w_up, w_down):
    n_t, top = expert_ids.shape
    n_e, d, ff = w_gate.shape
    peers = lax.axis_size("expert")
    ny = peers // 2
    replicas = nx * nz
    cap = n_t * top * 2 // (n_e * peers)
    scale = float(n_t * replicas * top // n_e) ** (-0.5)
    me = lax.axis_index("expert")
    place = lax.axis_index("dp")

    def to(a, dy, dc):
        perm = [(y * 2 + c, ((y + dy) % ny) * 2 + (c ^ dc)) for y in range(ny) for c in range(2)]
        return lax.ppermute(a, "expert", perm)

    tok = {(0, 0): with_meta(expert_ids.T, gate_fixed.T, tokens)}
    cot = {(0, 0): cotangent}
    tok[3, 0], cot[1, 0] = to(tok[0, 0], 1, 0), to(cot[0, 0], -1, 0)
    cot[3, 0], tok[1, 0] = to(cot[0, 0], 1, 0), to(tok[0, 0], -1, 0)
    tok[2, 0], cot[2, 0] = to(tok[3, 0], 1, 0), to(cot[1, 0], -1, 0)
    for dy in range(4):
        tok[dy, 1], cot[dy, 1] = to(tok[dy, 0], 0, 1), to(cot[dy, 0], 0, 1)
    order = [(dy, dc) for dy in (0, 1, 3, 2) for dc in range(2)]
    mine = me.reshape(1)
    near = pack(mine, [tok[r] for r in order[:6]], [cot[r] for r in order[:6]], cap, n_e)
    far = pack(mine, [tok[r] for r in order[6:]], [cot[r] for r in order[6:]], cap, n_e)
    chunk_order = lax.dynamic_index_in_dim(jnp.asarray(chunk_orders(nx, nz)), place, 0, keepdims=False)
    weights = (w_gate, w_up, w_down)
    y, c = me // 2, me % 2
    sources = jnp.stack([((y + dy) % ny) * 2 + (c + dc) % 2 for dy, dc in order])
    ret, send_a, keep_a = experts(0, chunk_order, sources, near, far, weights, [], cap, scale, replicas)
    ret, send_b, keep_b = experts(2, chunk_order, sources, near, far, weights, ret, cap, scale, replicas)
    total, last = reduce_grads((*send_a, *send_b), (*keep_a, *keep_b), nx, nz)
    back = lax.all_to_all(ret[0], "expert", split_axis=0, concat_axis=0, tiled=True)
    layer_out, input_grad = combine(expert_ids, gate_fixed, last[-1], back)
    total = jnp.concatenate(total, 0)
    return (layer_out, input_grad, total[:, :, :ff], total[:, :, ff : 2 * ff], total[:, :, 2 * ff :])


def solution(mesh):
    nx = 4
    nz = mesh.shape["dp"] // nx
    return jax.shard_map(
        functools.partial(shards, nx, nz),
        mesh=mesh,
        in_specs=(P(("dp", "expert"), None),) * 4 + (P("expert", None, None),) * 3,
        out_specs=(P(("dp", "expert"), None),) * 2 + (P("expert", "dp", None),) * 3,
        check_vma=False,
    )
```

```python
import functools

import jax
import jax.numpy as jnp
import numpy as np
from jax import lax
from jax.experimental import pallas as pl
from jax.experimental.pallas import tpu as pltpu
from jax.sharding import PartitionSpec as P

F32, BF16 = jnp.float32, jnp.bfloat16
META = 16


def dot(a, b, dims=((1,), (0,))):
    return lax.dot_general(a, b, (dims, ((), ())), preferred_element_type=F32)


ROOM = pltpu.CompilerParams(vmem_limit_bytes=56 * 2**20)
SCALARS = pl.BlockSpec(memory_space=pltpu.SMEM)


def whole(shape):
    return pl.BlockSpec(shape, lambda i: (0,) * len(shape))


def less_than(size, transposed):
    rows = lax.broadcasted_iota(jnp.int32, (size, size), 0)
    cols = lax.broadcasted_iota(jnp.int32, (size, size), 1)
    return ((cols < rows) if transposed else (rows < cols)).astype(F32).astype(BF16)


def meta_kernel(ids_ref, gate_ref, tok_ref, out_ref):
    n_t, d = tok_ref.shape
    ids, gate = ids_ref[...], gate_ref[...]
    high, low = gate // 256, gate % 256
    meta = jnp.concatenate([ids, high, low], 0).astype(F32)
    meta = jnp.concatenate([meta, jnp.zeros((META - 6, n_t), F32)], 0)
    out_ref[:n_t, :] = tok_ref[...]
    out_ref[n_t:, :n_t] = meta.astype(BF16)
    out_ref[n_t:, n_t:] = jnp.zeros((META, d - n_t), BF16)


def with_meta(ids, gate, tokens):
    n_t, d = tokens.shape
    return pl.pallas_call(
        meta_kernel,
        grid=(1,),
        in_specs=[whole(ids.shape), whole(gate.shape), whole(tokens.shape)],
        out_specs=whole((n_t + META, d)),
        out_shape=jax.ShapeDtypeStruct((n_t + META, d), BF16),
        compiler_params=ROOM,
        cost_estimate=pl.CostEstimate(flops=n_t * d, bytes_accessed=4 * n_t * d, transcendentals=0),
    )(ids, gate, tokens)


def pack_kernel(n, cap, n_e, me_ref, *refs):
    tok, cot = refs[:n], refs[n : 2 * n]
    rows_ref, grads_ref = refs[2 * n :]
    n_t = cot[0].shape[0]
    eid = (me_ref[0] * n_e + lax.broadcasted_iota(jnp.int32, (n_e, n_t), 0)).astype(F32)
    masks, gates = [], []
    for r in range(n):
        meta = tok[r][n_t : n_t + META, :n_t].astype(F32)
        row = lambda i: jnp.broadcast_to(meta[i : i + 1], (n_e, n_t))
        first, second = row(0) == eid, row(1) == eid
        g0 = (row(2) * 256.0 + row(4)) / 65536.0
        g1 = (row(3) * 256.0 + row(5)) / 65536.0
        masks.append(jnp.where(first | second, 1.0, 0.0))
        gates.append(jnp.where(first, g0, jnp.where(second, g1, 0.0)))
    mask = jnp.concatenate(masks, 0)
    rank = jnp.where(mask > 0.5, dot(mask.astype(BF16), less_than(n_t, False)), -1.0)
    slot = lax.broadcasted_iota(jnp.int32, (cap, n_t), 0).astype(F32)
    for r in range(n):
        hots, slot_gates = [], []
        for e in range(n_e):
            i = r * n_e + e
            hot = jnp.where(jnp.broadcast_to(rank[i : i + 1], (cap, n_t)) == slot, 1.0, 0.0)
            hots.append(hot)
            slot_gates.append(jnp.sum(hot * gates[r][e : e + 1], axis=1, keepdims=True))
        hot = jnp.concatenate(hots, 0).astype(BF16)
        slot_gate = jnp.concatenate(slot_gates, 0)
        rows = dot(hot, tok[r][:n_t, :]).astype(BF16)
        grads = (slot_gate * dot(hot, cot[r][...])).astype(BF16)
        for e in range(n_e):
            rows_ref[e, r * cap : (r + 1) * cap, :] = rows[e * cap : (e + 1) * cap]
            grads_ref[e, r * cap : (r + 1) * cap, :] = grads[e * cap : (e + 1) * cap]


def pack(me, tok, cot, cap, n_e):
    n, (n_t, d) = len(cot), cot[0].shape
    out = jax.ShapeDtypeStruct((n_e, n * cap, d), BF16)
    return pl.pallas_call(
        functools.partial(pack_kernel, n, cap, n_e),
        grid=(1,),
        in_specs=[SCALARS] + [whole(a.shape) for a in (*tok, *cot)],
        out_specs=[whole(out.shape)] * 2,
        out_shape=[out, out],
        compiler_params=ROOM,
        cost_estimate=pl.CostEstimate(
            flops=4 * n * n_e * cap * n_t * d, bytes_accessed=4 * n * (n_t + n_e * cap) * d, transcendentals=0
        ),
    )(me, *tok, *cot)


def grads_kernel(first, scale, place_ref, order_ref, near_x, far_x, near_g, far_g, wg_ref, wu_ref, wd_ref, *refs):
    saved, send, keep, acc = refs[0], refs[1:3], refs[3:5], refs[5:8]
    step = pl.program_id(0)
    x = jnp.concatenate([near_x[0], far_x[0]], 0)
    dy = jnp.concatenate([near_g[0], far_g[0]], 0)
    pre_gate, pre_up = dot(x, wg_ref[0]), dot(x, wu_ref[0])
    hidden_grad = dot(dy, wd_ref[0])
    sig = jax.nn.sigmoid(pre_gate)
    act = pre_gate * sig
    hidden = (act * pre_up).astype(BF16)
    gate_grad = (hidden_grad * pre_up * sig * (1.0 + pre_gate * (1.0 - sig))).astype(BF16)
    up_grad = (hidden_grad * act).astype(BF16)
    ff, half = hidden.shape[1], acc[0].shape[0] // 2
    for k, a in enumerate((hidden, gate_grad, up_grad)):
        saved[0, :, k * ff : (k + 1) * ff] = a
    shape = acc[0].shape
    acc[0][...] = (dot(x, gate_grad, ((0,), (0,))) * scale).reshape(shape)
    acc[1][...] = (dot(x, up_grad, ((0,), (0,))) * scale).reshape(shape)
    acc[2][...] = (dot(dy, hidden, ((0,), (0,))) * scale).reshape(shape)
    for i in range(2):

        @pl.when(step == i)
        def _(i=i):
            for p in range(2 * half):
                chunk = order_ref[place_ref[0], (first + i) * 2 * half + p]
                to = (send if p < half else keep)[i]
                for k in range(3):
                    to[p % half, :, k * ff : (k + 1) * ff] = acc[k][chunk].astype(BF16)


def expert_grads(first, place, order, near, far, weights, scale):
    n_e, d, ff = weights[0].shape
    replicas = order.shape[0]
    slots = near[0].shape[1] + far[0].shape[1]
    part = lambda a: pl.BlockSpec((1, *a.shape[1:]), lambda e: (first + e, 0, 0))
    rows = [near[0], far[0], near[1], far[1]]
    chunks = jax.ShapeDtypeStruct((replicas // 2, d // replicas, 3 * ff), BF16)
    out = pl.pallas_call(
        functools.partial(grads_kernel, first, scale),
        grid=(2,),
        in_specs=[SCALARS] * 2 + [part(a) for a in (*rows, *weights)],
        out_specs=[pl.BlockSpec((1, slots, 3 * ff), lambda e: (e, 0, 0))] + [whole(chunks.shape)] * 4,
        out_shape=[jax.ShapeDtypeStruct((2, slots, 3 * ff), BF16)] + [chunks] * 4,
        scratch_shapes=[pltpu.VMEM((replicas, d // replicas, ff), F32)] * 3,
        compiler_params=ROOM,
        cost_estimate=pl.CostEstimate(
            flops=24 * slots * d * ff, bytes_accessed=24 * d * ff + 8 * slots * d, transcendentals=2 * slots * ff
        ),
    )(place, order, *rows, *weights)
    return out[0], out[1:3], out[3:5]


def returns_kernel(cap, order, me_ref, saved_a, saved_b, wg_ref, wu_ref, wd_ref, ret):
    step = pl.program_id(0)
    half = pl.num_programs(0) // 2
    saved = jnp.where(step < half, saved_a[0], saved_b[0])
    ff = saved.shape[1] // 3
    hidden, gate_grad, up_grad = saved[:, :ff], saved[:, ff : 2 * ff], saved[:, 2 * ff :]
    out = dot(hidden, wd_ref[0], ((1,), (1,))).astype(BF16)
    entry = dot(gate_grad, wg_ref[0], ((1,), (1,))) + dot(up_grad, wu_ref[0], ((1,), (1,)))
    entry = entry.astype(BF16)
    me, ny = me_ref[0], ret.shape[0] // 2
    for r, (dy, dc) in enumerate(order):
        source = lax.rem(me // 2 + dy, ny) * 2 + lax.rem(me + dc, 2)
        ret[source, 0, 0] = out[r * cap : (r + 1) * cap]
        ret[source, 1, 0] = entry[r * cap : (r + 1) * cap]


def expert_returns(me, order, saved_a, saved_b, weights, cap):
    n_e, d, ff = weights[0].shape
    half, slots = n_e // 2, saved_a.shape[1]
    weight = pl.BlockSpec((1, d, ff), lambda e: (e, 0, 0))
    block = (1, slots, 3 * ff)
    return pl.pallas_call(
        functools.partial(returns_kernel, cap, order),
        grid=(n_e,),
        in_specs=[
            SCALARS,
            pl.BlockSpec(block, lambda e: (jnp.minimum(e, half - 1), 0, 0)),
            pl.BlockSpec(block, lambda e: (jnp.maximum(e - half, 0), 0, 0)),
        ]
        + [weight] * 3,
        out_specs=pl.BlockSpec((8, 2, 1, cap, d), lambda e: (0, 0, e, 0, 0)),
        out_shape=jax.ShapeDtypeStruct((8, 2, n_e, cap, d), BF16),
        compiler_params=ROOM,
        cost_estimate=pl.CostEstimate(
            flops=6 * n_e * slots * d * ff,
            bytes_accessed=6 * n_e * (d * ff + slots * ff) + 4 * n_e * slots * d,
            transcendentals=0,
        ),
    )(me, saved_a, saved_b, *weights)


def columns(a):
    a = a.astype(F32)
    return jnp.concatenate([a, jnp.zeros((8 - a.shape[0], a.shape[1]), F32)], 0).T


def combine_kernel(cap, ids_ref, gate_ref, _, ret, out_ref, grad_ref):
    n_t, count = ids_ref.shape[1], ret.shape[0] * ret.shape[2]
    eid = lax.broadcasted_iota(jnp.int32, (n_t, count), 1).astype(F32)
    ids = columns(ids_ref[...])
    first, second = ids[:, 0:1] == eid, ids[:, 1:2] == eid
    mask = jnp.where(first | second, 1.0, 0.0).astype(BF16)
    rank = dot(less_than(n_t, True), mask)
    rows = lax.broadcasted_iota(jnp.int32, (count, count * cap), 0)
    cols = lax.broadcasted_iota(jnp.int32, (count, count * cap), 1)
    spread = jnp.where(cols // cap == rows, 1.0, 0.0).astype(BF16)
    slot = (lax.broadcasted_iota(jnp.int32, (n_t, count * cap), 1) % cap).astype(F32)
    hots = [
        jnp.where(dot(jnp.where(m, rank, -1.0).astype(BF16), spread) == slot, 1.0, 0.0)
        for m in (first, second)
    ]
    both = (hots[0] + hots[1]).astype(BF16)
    hots = [h.astype(BF16) for h in hots]
    outs = ret[:, 0].reshape(count * cap, ret.shape[-1])
    grads = ret[:, 1].reshape(count * cap, ret.shape[-1])
    gate = columns(gate_ref[...]) / 65536.0
    total = gate[:, 0:1] * dot(hots[0], outs) + gate[:, 1:2] * dot(hots[1], outs)
    out_ref[...] = total.astype(BF16)
    grad_ref[...] = dot(both, grads).astype(BF16)


def combine(ids, gate, after, ret):
    peers, _, n_e, cap, d = ret.shape
    n_t = ids.shape[1]
    row = jax.ShapeDtypeStruct((n_t, d), BF16)
    return pl.pallas_call(
        functools.partial(combine_kernel, cap),
        grid=(1,),
        in_specs=[whole(ids.shape), whole(gate.shape), pl.BlockSpec(memory_space=pl.ANY), whole(ret.shape)],
        out_specs=[whole(row.shape)] * 2,
        out_shape=[row, row],
        compiler_params=pltpu.CompilerParams(vmem_limit_bytes=24 * 2**20),
        cost_estimate=pl.CostEstimate(
            flops=6 * n_t * d * peers * n_e * cap, bytes_accessed=40 * n_t * d, transcendentals=0
        ),
    )(ids, gate, after, ret)


PLANS = (
    ("xp", "xq", "zp", "zq", "zf"),
    ("xq", "xp", "zq", "zp", "zg"),
    ("zp", "zq", "xp", "xq", "zf"),
    ("zq", "zp", "xq", "xp", "zg"),
)
FAR = {"zf": (3, 6, 5, 0, 7, 2, 1, 4), "zg": (5, 4, 7, 6, 1, 0, 3, 2)}


def partners(kind, nx, nz):
    out = []
    for x in range(nx):
        for z in range(nz):
            at, n = (x, nx) if kind[0] == "x" else (z, nz)
            if kind in FAR:
                at = FAR[kind][at]
            elif kind[1] == "p":
                at = at ^ 1
            else:
                at = (at + 1) % n if at % 2 else (at - 1) % n
            out.append(at * nz + z if kind[0] == "x" else x * nz + at)
    return out


def chunk_orders(nx, nz):
    plans = []
    for plan in PLANS:
        held = [[i] for i in range(nx * nz)]
        for kind in reversed(plan):
            with_ = partners(kind, nx, nz)
            held = [held[with_[i]] + held[i] for i in range(nx * nz)]
        plans.append(held)
    return np.asarray(plans, np.int32).swapaxes(0, 1)


def reduce_grads(send, keep, nx, nz):
    send, keep = list(send), list(keep)
    swap = lambda a, kind: lax.ppermute(a, "dp", list(enumerate(partners(kind, nx, nz))))
    steps = len(PLANS[0])
    for k in range(steps):
        got = [swap(send[v], PLANS[v][k]) for v in range(4)]
        if k == steps - 1:
            return keep, got, send
        half = keep[0].shape[0] // 2
        for v in range(4):
            send[v] = (keep[v][:half].astype(F32) + got[v][:half].astype(F32)).astype(BF16)
            keep[v] = (keep[v][half:].astype(F32) + got[v][half:].astype(F32)).astype(BF16)


def shards(nx, nz, tokens, expert_ids, gate_fixed, cotangent, w_gate, w_up, w_down):
    n_t, top = expert_ids.shape
    n_e, d, ff = w_gate.shape
    peers = lax.axis_size("expert")
    ny = peers // 2
    replicas = nx * nz
    cap = n_t * top * 2 // (n_e * peers)
    scale = float(n_t * replicas * top // n_e) ** (-0.5)
    me = lax.axis_index("expert")
    place = lax.axis_index("dp")

    def to(a, dy, dc):
        perm = [(y * 2 + c, ((y + dy) % ny) * 2 + (c ^ dc)) for y in range(ny) for c in range(2)]
        return lax.ppermute(a, "expert", perm)

    ids, gate = expert_ids.T, gate_fixed.T
    tok = {(0, 0): with_meta(ids, gate, tokens)}
    cot = {(0, 0): cotangent}
    tok[3, 0], cot[1, 0] = to(tok[0, 0], 1, 0), to(cotangent, -1, 0)
    tok[0, 1], cot[0, 1] = to(tok[0, 0], 0, 1), to(cotangent, 0, 1)
    own_t, own_c, tok[3, 0], cot[1, 0] = lax.optimization_barrier((tok[0, 0], cotangent, tok[3, 0], cot[1, 0]))
    cot[3, 0], tok[1, 0] = to(own_c, 1, 0), to(own_t, -1, 0)
    tok[3, 1], cot[1, 1] = to(tok[3, 0], 0, 1), to(cot[1, 0], 0, 1)
    by_t, by_c, cot[3, 0], tok[1, 0] = lax.optimization_barrier((tok[3, 0], cot[1, 0], cot[3, 0], tok[1, 0]))
    tok[2, 0], cot[2, 0] = to(by_t, 1, 0), to(by_c, -1, 0)
    cot[3, 1], tok[1, 1] = to(cot[3, 0], 0, 1), to(tok[1, 0], 0, 1)
    order = tuple((dy, dc) for dy in (0, 1, 3, 2) for dc in range(2))
    mine, here = me.reshape(1), place.reshape(1)
    near = pack(mine, [tok[r] for r in order[:6]], [cot[r] for r in order[:6]], cap, n_e)
    near, tok[2, 0], cot[2, 0] = lax.optimization_barrier((near, tok[2, 0], cot[2, 0]))
    tok[2, 1], cot[2, 1] = to(tok[2, 0], 0, 1), to(cot[2, 0], 0, 1)
    far = pack(mine, [tok[r] for r in order[6:]], [cot[r] for r in order[6:]], cap, n_e)
    chunks = jnp.asarray(chunk_orders(nx, nz).reshape(replicas, -1))
    weights = (w_gate, w_up, w_down)
    saved_a, send_a, keep_a = expert_grads(0, here, chunks, near, far, weights, scale)
    saved_b, send_b, keep_b = expert_grads(2, here, chunks, near, far, weights, scale)
    keep, got, last = reduce_grads((*send_a, *send_b), (*keep_a, *keep_b), nx, nz)
    ret = expert_returns(mine, order, saved_a, saved_b, weights, cap)
    back = lax.all_to_all(ret, "expert", split_axis=0, concat_axis=0, tiled=True)
    layer_out, input_grad = combine(ids, gate, last[-1], back)
    got, layer_out = lax.optimization_barrier((got, layer_out))
    total = jnp.concatenate([a.astype(F32) + b.astype(F32) for a, b in zip(keep, got)], 0)
    return (layer_out, input_grad, total[:, :, :ff], total[:, :, ff : 2 * ff], total[:, :, 2 * ff :])


def solution(mesh):
    nx = 4
    nz = mesh.shape["dp"] // nx
    return jax.shard_map(
        functools.partial(shards, nx, nz),
        mesh=mesh,
        in_specs=(P(("dp", "expert"), None),) * 4 + (P("expert", None, None),) * 3,
        out_specs=(P(("dp", "expert"), None),) * 2 + (P("expert", "dp", None),) * 3,
        check_vma=False,
    )
```

```python
import functools

import jax
import jax.numpy as jnp
import numpy as np
from jax import lax
from jax.experimental import pallas as pl
from jax.experimental.pallas import tpu as pltpu
from jax.sharding import PartitionSpec as P

F32, BF16 = jnp.float32, jnp.bfloat16
META = 16


def dot(a, b, dims=((1,), (0,))):
    return lax.dot_general(a, b, (dims, ((), ())), preferred_element_type=F32)


ROOM = pltpu.CompilerParams(vmem_limit_bytes=56 * 2**20)
SCALARS = pl.BlockSpec(memory_space=pltpu.SMEM)


def whole(shape):
    return pl.BlockSpec(shape, lambda i: (0,) * len(shape))


def less_than(size, transposed):
    rows = lax.broadcasted_iota(jnp.int32, (size, size), 0)
    cols = lax.broadcasted_iota(jnp.int32, (size, size), 1)
    return ((cols < rows) if transposed else (rows < cols)).astype(F32).astype(BF16)


def meta_kernel(ids_ref, gate_ref, tok_ref, out_ref):
    n_t, d = tok_ref.shape
    ids, gate = ids_ref[...], gate_ref[...]
    high, low = gate // 256, gate % 256
    meta = jnp.concatenate([ids, high, low], 0).astype(F32)
    meta = jnp.concatenate([meta, jnp.zeros((META - 6, n_t), F32)], 0)
    out_ref[:n_t, :] = tok_ref[...]
    out_ref[n_t:, :n_t] = meta.astype(BF16)
    out_ref[n_t:, n_t:] = jnp.zeros((META, d - n_t), BF16)


def with_meta(ids, gate, tokens):
    n_t, d = tokens.shape
    return pl.pallas_call(
        meta_kernel,
        grid=(1,),
        in_specs=[whole(ids.shape), whole(gate.shape), whole(tokens.shape)],
        out_specs=whole((n_t + META, d)),
        out_shape=jax.ShapeDtypeStruct((n_t + META, d), BF16),
        compiler_params=ROOM,
        cost_estimate=pl.CostEstimate(flops=n_t * d, bytes_accessed=4 * n_t * d, transcendentals=0),
    )(ids, gate, tokens)


def pack_kernel(n, cap, n_e, me_ref, *refs):
    tok, cot = refs[:n], refs[n : 2 * n]
    rows_ref, grads_ref = refs[-2:]
    n_t = cot[0].shape[0]
    eid = (me_ref[0] * n_e + lax.broadcasted_iota(jnp.int32, (n_e, n_t), 0)).astype(F32)
    masks, gates = [], []
    for r in range(n):
        meta = tok[r][n_t : n_t + META, :n_t].astype(F32)
        row = lambda i: jnp.broadcast_to(meta[i : i + 1], (n_e, n_t))
        first, second = row(0) == eid, row(1) == eid
        g0 = (row(2) * 256.0 + row(4)) / 65536.0
        g1 = (row(3) * 256.0 + row(5)) / 65536.0
        masks.append(jnp.where(first | second, 1.0, 0.0))
        gates.append(jnp.where(first, g0, jnp.where(second, g1, 0.0)))
    mask = jnp.concatenate(masks, 0)
    rank = jnp.where(mask > 0.5, dot(mask.astype(BF16), less_than(n_t, False)), -1.0)
    slot = lax.broadcasted_iota(jnp.int32, (cap, n_t), 0).astype(F32)
    for r in range(n):
        hots, slot_gates = [], []
        for e in range(n_e):
            i = r * n_e + e
            hot = jnp.where(jnp.broadcast_to(rank[i : i + 1], (cap, n_t)) == slot, 1.0, 0.0)
            hots.append(hot)
            slot_gates.append(jnp.sum(hot * gates[r][e : e + 1], axis=1, keepdims=True))
        hot = jnp.concatenate(hots, 0).astype(BF16)
        slot_gate = jnp.concatenate(slot_gates, 0)
        rows = dot(hot, tok[r][:n_t, :]).astype(BF16)
        grads = (slot_gate * dot(hot, cot[r][...])).astype(BF16)
        for e in range(n_e):
            rows_ref[e, r * cap : (r + 1) * cap, :] = rows[e * cap : (e + 1) * cap]
            grads_ref[e, r * cap : (r + 1) * cap, :] = grads[e * cap : (e + 1) * cap]


def pack(me, tok, cot, cap, n_e, before=()):
    n, (n_t, d) = len(cot), cot[0].shape
    out = jax.ShapeDtypeStruct((n_e, 8 * cap, d), BF16)
    at = 8 // n - 1 if before else 0
    return pl.pallas_call(
        functools.partial(pack_kernel, n, cap, n_e),
        grid=(1,),
        in_specs=[SCALARS]
        + [whole(a.shape) for a in (*tok, *cot)]
        + [pl.BlockSpec(memory_space=pl.ANY)] * len(before),
        out_specs=[pl.BlockSpec((n_e, n * cap, d), lambda i: (0, at, 0))] * 2,
        out_shape=[out, out],
        input_output_aliases={2 * n + 1 + i: i for i in range(len(before))},
        compiler_params=ROOM,
        cost_estimate=pl.CostEstimate(
            flops=4 * n * n_e * cap * n_t * d, bytes_accessed=4 * n * (n_t + n_e * cap) * d, transcendentals=0
        ),
    )(me, *tok, *cot, *before)


def grads_kernel(scale, place_ref, order_ref, x_ref, dy_ref, wg_ref, wu_ref, wd_ref, *refs):
    n_e = pl.num_programs(0)
    saved, send, keep, acc = refs[0], refs[1:5], refs[5:9], refs[9]
    step = pl.program_id(0)
    x, dy = x_ref[0], dy_ref[0]
    pre_gate, pre_up = dot(x, wg_ref[0]), dot(x, wu_ref[0])
    hidden_grad = dot(dy, wd_ref[0])
    sig = jax.nn.sigmoid(pre_gate)
    act = pre_gate * sig
    hidden = (act * pre_up).astype(BF16)
    gate_grad = (hidden_grad * pre_up * sig * (1.0 + pre_gate * (1.0 - sig))).astype(BF16)
    up_grad = (hidden_grad * act).astype(BF16)
    ff, replicas = hidden.shape[1], acc.shape[0]
    half = replicas // 2
    both = jnp.concatenate([gate_grad, up_grad], 1)
    saved[0, :, :ff] = hidden
    saved[0, :, ff:] = both
    acc[:, :, : 2 * ff] = (dot(x, both, ((0,), (0,))) * scale).reshape(replicas, -1, 2 * ff)
    acc[:, :, 2 * ff :] = (dot(dy, hidden, ((0,), (0,))) * scale).reshape(replicas, -1, ff)
    for i in range(4):

        @pl.when(step == i)
        def _(i=i):
            for p in range(replicas):
                chunk = order_ref[place_ref[0], i * replicas + p]
                (send if p < half else keep)[i][p % half] = acc[chunk].astype(BF16)


def expert_grads(place, order, rows, grads, weights, scale):
    n_e, d, ff = weights[0].shape
    replicas = order.shape[0]
    slots = rows.shape[1]
    part = lambda a: pl.BlockSpec((1, *a.shape[1:]), lambda e: (e, 0, 0))
    saved = jax.ShapeDtypeStruct((n_e, slots, 3 * ff), BF16)
    chunks = jax.ShapeDtypeStruct((replicas // 2, d // replicas, 3 * ff), BF16)
    out = pl.pallas_call(
        functools.partial(grads_kernel, scale),
        grid=(n_e,),
        in_specs=[SCALARS] * 2 + [part(a) for a in (rows, grads, *weights)],
        out_specs=[part(saved)] + [whole(chunks.shape)] * 8,
        out_shape=[saved] + [chunks] * 8,
        scratch_shapes=[pltpu.VMEM((replicas, d // replicas, 3 * ff), F32)],
        compiler_params=ROOM,
        cost_estimate=pl.CostEstimate(
            flops=12 * n_e * slots * d * ff,
            bytes_accessed=n_e * (12 * d * ff + 4 * slots * d),
            transcendentals=n_e * slots * ff,
        ),
    )(place, order, rows, grads, *weights)
    return out[0], out[1:5], out[5:9]


def returns_kernel(cap, order, me_ref, saved_ref, wg_ref, wu_ref, wd_ref, ret):
    saved = saved_ref[0]
    ff = saved.shape[1] // 3
    hidden, gate_grad, up_grad = saved[:, :ff], saved[:, ff : 2 * ff], saved[:, 2 * ff :]
    out = dot(hidden, wd_ref[0], ((1,), (1,))).astype(BF16)
    entry = dot(gate_grad, wg_ref[0], ((1,), (1,))) + dot(up_grad, wu_ref[0], ((1,), (1,)))
    entry = entry.astype(BF16)
    me, ny = me_ref[0], ret.shape[0] // 2
    for r, (dy, dc) in enumerate(order):
        source = lax.rem(me // 2 + dy, ny) * 2 + lax.rem(me + dc, 2)
        ret[source, 0, 0] = out[r * cap : (r + 1) * cap]
        ret[source, 1, 0] = entry[r * cap : (r + 1) * cap]


def expert_returns(me, order, saved, weights, cap):
    n_e, d, ff = weights[0].shape
    slots = saved.shape[1]
    part = lambda a: pl.BlockSpec((1, *a.shape[1:]), lambda e: (e, 0, 0))
    return pl.pallas_call(
        functools.partial(returns_kernel, cap, order),
        grid=(n_e,),
        in_specs=[SCALARS] + [part(a) for a in (saved, *weights)],
        out_specs=pl.BlockSpec((8, 2, 1, cap, d), lambda e: (0, 0, e, 0, 0)),
        out_shape=jax.ShapeDtypeStruct((8, 2, n_e, cap, d), BF16),
        compiler_params=ROOM,
        cost_estimate=pl.CostEstimate(
            flops=6 * n_e * slots * d * ff,
            bytes_accessed=6 * n_e * (d * ff + slots * ff) + 4 * n_e * slots * d,
            transcendentals=0,
        ),
    )(me, saved, *weights)


def columns(a):
    a = a.astype(F32)
    return jnp.concatenate([a, jnp.zeros((8 - a.shape[0], a.shape[1]), F32)], 0).T


def combine_kernel(cap, ids_ref, gate_ref, _, ret, out_ref, grad_ref):
    n_t, count = ids_ref.shape[1], ret.shape[0] * ret.shape[2]
    eid = lax.broadcasted_iota(jnp.int32, (n_t, count), 1).astype(F32)
    ids = columns(ids_ref[...])
    first, second = ids[:, 0:1] == eid, ids[:, 1:2] == eid
    mask = jnp.where(first | second, 1.0, 0.0).astype(BF16)
    rank = dot(less_than(n_t, True), mask)
    rows = lax.broadcasted_iota(jnp.int32, (count, count * cap), 0)
    cols = lax.broadcasted_iota(jnp.int32, (count, count * cap), 1)
    spread = jnp.where(cols // cap == rows, 1.0, 0.0).astype(BF16)
    slot = (lax.broadcasted_iota(jnp.int32, (n_t, count * cap), 1) % cap).astype(F32)
    hots = [
        jnp.where(dot(jnp.where(m, rank, -1.0).astype(BF16), spread) == slot, 1.0, 0.0)
        for m in (first, second)
    ]
    both = (hots[0] + hots[1]).astype(BF16)
    hots = [h.astype(BF16) for h in hots]
    outs = ret[:, 0].reshape(count * cap, ret.shape[-1])
    grads = ret[:, 1].reshape(count * cap, ret.shape[-1])
    gate = columns(gate_ref[...]) / 65536.0
    total = gate[:, 0:1] * dot(hots[0], outs) + gate[:, 1:2] * dot(hots[1], outs)
    out_ref[...] = total.astype(BF16)
    grad_ref[...] = dot(both, grads).astype(BF16)


def combine(ids, gate, after, ret):
    peers, _, n_e, cap, d = ret.shape
    n_t = ids.shape[1]
    row = jax.ShapeDtypeStruct((n_t, d), BF16)
    return pl.pallas_call(
        functools.partial(combine_kernel, cap),
        grid=(1,),
        in_specs=[whole(ids.shape), whole(gate.shape), pl.BlockSpec(memory_space=pl.ANY), whole(ret.shape)],
        out_specs=[whole(row.shape)] * 2,
        out_shape=[row, row],
        compiler_params=pltpu.CompilerParams(vmem_limit_bytes=24 * 2**20),
        cost_estimate=pl.CostEstimate(
            flops=6 * n_t * d * peers * n_e * cap, bytes_accessed=40 * n_t * d, transcendentals=0
        ),
    )(ids, gate, after, ret)


PLANS = (
    ("xp", "xq", "zp", "zq", "zf"),
    ("xq", "xp", "zp", "zq", "zf"),
    ("zp", "zq", "xp", "xq", "zf"),
    ("zq", "zp", "xp", "xq", "zg"),
)
FAR = {"zf": (3, 6, 5, 0, 7, 2, 1, 4), "zg": (5, 4, 7, 6, 1, 0, 3, 2)}


def partners(kind, nx, nz):
    out = []
    for x in range(nx):
        for z in range(nz):
            at, n = (x, nx) if kind[0] == "x" else (z, nz)
            if kind in FAR:
                at = FAR[kind][at]
            elif kind[1] == "p":
                at = at ^ 1
            else:
                at = (at + 1) % n if at % 2 else (at - 1) % n
            out.append(at * nz + z if kind[0] == "x" else x * nz + at)
    return out


def chunk_orders(nx, nz):
    plans = []
    for plan in PLANS:
        held = [[i] for i in range(nx * nz)]
        for kind in reversed(plan):
            with_ = partners(kind, nx, nz)
            held = [held[with_[i]] + held[i] for i in range(nx * nz)]
        plans.append(held)
    return np.asarray(plans, np.int32).swapaxes(0, 1)


def halve_kernel(n, plans, *refs):
    keep, got, out = refs[:n], refs[n : 2 * n], refs[2 * n :]
    at = 0
    for k_ref, g_ref in zip(keep, got):
        count = k_ref.shape[0] // plans
        half = count // 2
        for v in range(plans):
            for i, ref in enumerate((out[:-1][at // half] if len(out) > 2 else out[0], out[-1])):
                rows = pl.ds(v * count + i * half, half)
                to = 0 if len(out) > 2 and i == 0 else at
                ref[to : to + half] = (k_ref[rows].astype(F32) + g_ref[rows].astype(F32)).astype(BF16)
            at += half


def halve(keep, got, plans=1, apart=False):
    total = sum(a.shape[0] for a in keep) // 2
    shape = lambda count: jax.ShapeDtypeStruct((count, *keep[0].shape[1:]), BF16)
    n = len(keep)
    sends = [shape(total // (n * plans))] * (n * plans) if apart else [shape(total)]
    vmem = pl.BlockSpec(memory_space=pltpu.VMEM)
    out = pl.pallas_call(
        functools.partial(halve_kernel, n, plans),
        in_specs=[vmem] * (2 * n),
        out_specs=[vmem] * (len(sends) + 1),
        out_shape=[*sends, shape(total)],
        compiler_params=pltpu.CompilerParams(vmem_limit_bytes=8 * 2**20),
        cost_estimate=pl.CostEstimate(
            flops=2 * total * keep[0][0].size, bytes_accessed=12 * total * keep[0][0].size, transcendentals=0
        ),
    )(*keep, *got)
    return out[:-1], out[-1]


def halve_plain(keep, got, plans=1, apart=False):
    sends, kept = [], []
    for k, g in zip(keep, got):
        count = k.shape[0] // plans
        half = count // 2
        for v in range(plans):
            a, b, c = v * count, v * count + half, (v + 1) * count
            sends.append((k[a:b].astype(F32) + g[a:b].astype(F32)).astype(BF16))
            kept.append((k[b:c].astype(F32) + g[b:c].astype(F32)).astype(BF16))
    join = lambda a: a[0] if len(a) == 1 else jnp.concatenate(a, 0)
    return (sends if apart else [join(sends)]), join(kept)


def reduce_grads(send, keep, nx, nz):
    swap = lambda a, kind: lax.ppermute(a, "dp", list(enumerate(partners(kind, nx, nz))))
    got = [swap(send[v], PLANS[v][0]) for v in range(4)]
    first = [halve_plain([keep[v]], [got[v]]) for v in range(4)]
    got = [swap(first[v][0][0], PLANS[v][1]) for v in range(4)]
    terms, sends = [], []
    for a, b in ((0, 1), (2, 3)):
        sent, kept = halve([first[a][1], first[b][1]], [got[a], got[b]])
        sent, kept = halve([kept], [swap(sent[0], PLANS[a][2])], 2)
        apart = PLANS[a][4] != PLANS[b][4]
        sent, kept = halve([kept], [swap(sent[0], PLANS[a][3])], 2, apart)
        last = [swap(sent[i], PLANS[v][4]) for i, v in enumerate((a, b)[: len(sent)])]
        terms.append((kept, last))
        sends += sent
    return [k for k, _ in terms], [g for _, g in terms], sends


def shards(nx, nz, tokens, expert_ids, gate_fixed, cotangent, w_gate, w_up, w_down):
    n_t, top = expert_ids.shape
    n_e, d, ff = w_gate.shape
    peers = lax.axis_size("expert")
    ny = peers // 2
    replicas = nx * nz
    cap = n_t * top * 2 // (n_e * peers)
    scale = float(n_t * replicas * top // n_e) ** (-0.5)
    me = lax.axis_index("expert")
    place = lax.axis_index("dp")

    def to(a, dy, dc):
        perm = [(y * 2 + c, ((y + dy) % ny) * 2 + (c ^ dc)) for y in range(ny) for c in range(2)]
        return lax.ppermute(a, "expert", perm)

    ids, gate = expert_ids.T, gate_fixed.T
    tok = {(0, 0): with_meta(ids, gate, tokens)}
    cot = {(0, 0): cotangent}
    cot[3, 0], cot[1, 0] = to(cotangent, 1, 0), to(cotangent, -1, 0)
    tok[0, 1], cot[0, 1] = to(tok[0, 0], 0, 1), to(cotangent, 0, 1)
    own, cot[3, 0], cot[1, 0] = lax.optimization_barrier((tok[0, 0], cot[3, 0], cot[1, 0]))
    tok[3, 0], tok[1, 0] = to(own, 1, 0), to(own, -1, 0)
    cot[3, 1], cot[1, 1] = to(cot[3, 0], 0, 1), to(cot[1, 0], 0, 1)
    by_c, tok[3, 0], tok[1, 0] = lax.optimization_barrier((cot[3, 0], tok[3, 0], tok[1, 0]))
    cot[2, 0], tok[2, 0] = to(by_c, 1, 0), to(tok[1, 0], -1, 0)
    tok[3, 1], tok[1, 1] = to(tok[3, 0], 0, 1), to(tok[1, 0], 0, 1)
    order = tuple((dy, dc) for dy in (0, 1, 3, 2) for dc in range(2))
    mine, here = me.reshape(1), place.reshape(1)
    near = pack(mine, [tok[r] for r in order[:6]], [cot[r] for r in order[:6]], cap, n_e)
    near, tok[2, 0], cot[2, 0] = lax.optimization_barrier((near, tok[2, 0], cot[2, 0]))
    tok[2, 1], cot[2, 1] = to(tok[2, 0], 0, 1), to(cot[2, 0], 0, 1)
    rows, grads = pack(mine, [tok[r] for r in order[6:]], [cot[r] for r in order[6:]], cap, n_e, near)
    chunks = jnp.asarray(chunk_orders(nx, nz).reshape(replicas, -1))
    weights = (w_gate, w_up, w_down)
    saved, send, keep = expert_grads(here, chunks, rows, grads, weights, scale)
    keep, got, last = reduce_grads(send, keep, nx, nz)
    ret = expert_returns(mine, order, saved, weights, cap)
    back = lax.all_to_all(ret, "expert", split_axis=0, concat_axis=0, tiled=True)
    layer_out, input_grad = combine(ids, gate, last[-1], back)
    got, layer_out = lax.optimization_barrier((got, layer_out))
    total = [k.astype(F32) + jnp.concatenate(g, 0).astype(F32) for k, g in zip(keep, got)]
    total = jnp.concatenate(total, 0)
    return (layer_out, input_grad, total[:, :, :ff], total[:, :, ff : 2 * ff], total[:, :, 2 * ff :])


def solution(mesh):
    nx = 4
    nz = mesh.shape["dp"] // nx
    return jax.shard_map(
        functools.partial(shards, nx, nz),
        mesh=mesh,
        in_specs=(P(("dp", "expert"), None),) * 4 + (P("expert", None, None),) * 3,
        out_specs=(P(("dp", "expert"), None),) * 2 + (P("expert", "dp", None),) * 3,
        check_vma=False,
    )
```

```python
import functools

import jax
import jax.numpy as jnp
import numpy as np
from jax import lax
from jax.experimental import pallas as pl
from jax.experimental.pallas import tpu as pltpu
from jax.sharding import PartitionSpec as P

F32, BF16 = jnp.float32, jnp.bfloat16
META = 16


def dot(a, b, dims=((1,), (0,))):
    return lax.dot_general(a, b, (dims, ((), ())), preferred_element_type=F32)


ROOM = pltpu.CompilerParams(vmem_limit_bytes=61 * 2**20)
SCALARS = pl.BlockSpec(memory_space=pltpu.SMEM)


def whole(shape):
    return pl.BlockSpec(shape, lambda i: (0,) * len(shape))


def less_than(size, transposed):
    rows = lax.broadcasted_iota(jnp.int32, (size, size), 0)
    cols = lax.broadcasted_iota(jnp.int32, (size, size), 1)
    return ((cols < rows) if transposed else (rows < cols)).astype(F32).astype(BF16)


def meta_kernel(ids_ref, gate_ref, tok_ref, out_ref):
    n_t, d = tok_ref.shape
    ids, gate = ids_ref[...], gate_ref[...]
    high, low = gate // 256, gate % 256
    meta = jnp.concatenate([ids, high, low], 0).astype(F32)
    meta = jnp.concatenate([meta, jnp.zeros((META - 6, n_t), F32)], 0)
    out_ref[:n_t, :] = tok_ref[...]
    out_ref[n_t:, :n_t] = meta.astype(BF16)
    out_ref[n_t:, n_t:] = jnp.zeros((META, d - n_t), BF16)


def with_meta(ids, gate, tokens):
    n_t, d = tokens.shape
    return pl.pallas_call(
        meta_kernel,
        grid=(1,),
        in_specs=[whole(ids.shape), whole(gate.shape), whole(tokens.shape)],
        out_specs=whole((n_t + META, d)),
        out_shape=jax.ShapeDtypeStruct((n_t + META, d), BF16),
        compiler_params=ROOM,
        cost_estimate=pl.CostEstimate(flops=n_t * d, bytes_accessed=4 * n_t * d, transcendentals=0),
    )(ids, gate, tokens)


def pack_kernel(n, cap, n_e, me_ref, *refs):
    tok, cot = refs[:n], refs[n : 2 * n]
    rows_ref, grads_ref = refs[-2:]
    n_t = cot[0].shape[0]
    eid = (me_ref[0] * n_e + lax.broadcasted_iota(jnp.int32, (n_e, n_t), 0)).astype(F32)
    masks, gates = [], []
    for r in range(n):
        meta = tok[r][n_t : n_t + META, :n_t].astype(F32)
        row = lambda i: jnp.broadcast_to(meta[i : i + 1], (n_e, n_t))
        first, second = row(0) == eid, row(1) == eid
        g0 = (row(2) * 256.0 + row(4)) / 65536.0
        g1 = (row(3) * 256.0 + row(5)) / 65536.0
        masks.append(jnp.where(first | second, 1.0, 0.0))
        gates.append(jnp.where(first, g0, jnp.where(second, g1, 0.0)))
    mask = jnp.concatenate(masks, 0)
    rank = jnp.where(mask > 0.5, dot(mask.astype(BF16), less_than(n_t, False)), -1.0)
    slot = lax.broadcasted_iota(jnp.int32, (cap, n_t), 0).astype(F32)
    for r in range(n):
        hots, slot_gates = [], []
        for e in range(n_e):
            i = r * n_e + e
            hot = jnp.where(jnp.broadcast_to(rank[i : i + 1], (cap, n_t)) == slot, 1.0, 0.0)
            hots.append(hot)
            slot_gates.append(jnp.sum(hot * gates[r][e : e + 1], axis=1, keepdims=True))
        hot = jnp.concatenate(hots, 0).astype(BF16)
        slot_gate = jnp.concatenate(slot_gates, 0)
        rows = dot(hot, tok[r][:n_t, :]).astype(BF16)
        grads = (slot_gate * dot(hot, cot[r][...])).astype(BF16)
        for e in range(n_e):
            rows_ref[e, r * cap : (r + 1) * cap, :] = rows[e * cap : (e + 1) * cap]
            grads_ref[e, r * cap : (r + 1) * cap, :] = grads[e * cap : (e + 1) * cap]


def pack(me, tok, cot, cap, n_e, before=()):
    n, (n_t, d) = len(cot), cot[0].shape
    out = jax.ShapeDtypeStruct((n_e, 8 * cap, d), BF16)
    at = 8 // n - 1 if before else 0
    return pl.pallas_call(
        functools.partial(pack_kernel, n, cap, n_e),
        grid=(1,),
        in_specs=[SCALARS]
        + [whole(a.shape) for a in (*tok, *cot)]
        + [pl.BlockSpec(memory_space=pl.ANY)] * len(before),
        out_specs=[pl.BlockSpec((n_e, n * cap, d), lambda i: (0, at, 0))] * 2,
        out_shape=[out, out],
        input_output_aliases={2 * n + 1 + i: i for i in range(len(before))},
        compiler_params=ROOM,
        cost_estimate=pl.CostEstimate(
            flops=4 * n * n_e * cap * n_t * d, bytes_accessed=4 * n * (n_t + n_e * cap) * d, transcendentals=0
        ),
    )(me, *tok, *cot, *before)


def grads_kernel(scale, place_ref, order_ref, x_ref, dy_ref, wg_ref, wu_ref, wd_ref, *refs):
    n_e = pl.num_programs(0)
    saved, send, keep, acc = refs[0], refs[1:5], refs[5:9], refs[9]
    step = pl.program_id(0)
    x, dy = x_ref[0], dy_ref[0]
    pre_gate, pre_up = dot(x, wg_ref[0]), dot(x, wu_ref[0])
    hidden_grad = dot(dy, wd_ref[0])
    sig = jax.nn.sigmoid(pre_gate)
    act = pre_gate * sig
    hidden = (act * pre_up).astype(BF16)
    gate_grad = (hidden_grad * pre_up * sig * (1.0 + pre_gate * (1.0 - sig))).astype(BF16)
    up_grad = (hidden_grad * act).astype(BF16)
    ff, replicas = hidden.shape[1], acc.shape[0]
    half = replicas // 2
    both = jnp.concatenate([gate_grad, up_grad], 1)
    saved[0, :, :ff] = hidden
    saved[0, :, ff:] = both
    acc[:, :, : 2 * ff] = (dot(x, both, ((0,), (0,))) * scale).reshape(replicas, -1, 2 * ff)
    acc[:, :, 2 * ff :] = (dot(dy, hidden, ((0,), (0,))) * scale).reshape(replicas, -1, ff)
    for i in range(4):

        @pl.when(step == i)
        def _(i=i):
            for p in range(replicas):
                chunk = order_ref[place_ref[0], i * replicas + p]
                (send if p < half else keep)[i][p % half] = acc[chunk].astype(BF16)


def expert_grads(place, order, rows, grads, weights, scale):
    n_e, d, ff = weights[0].shape
    replicas = order.shape[0]
    slots = rows.shape[1]
    part = lambda a: pl.BlockSpec((1, *a.shape[1:]), lambda e: (e, 0, 0))
    saved = jax.ShapeDtypeStruct((n_e, slots, 3 * ff), BF16)
    chunks = jax.ShapeDtypeStruct((replicas // 2, d // replicas, 3 * ff), BF16)
    out = pl.pallas_call(
        functools.partial(grads_kernel, scale),
        grid=(n_e,),
        in_specs=[SCALARS] * 2 + [part(a) for a in (rows, grads, *weights)],
        out_specs=[part(saved)] + [whole(chunks.shape)] * 8,
        out_shape=[saved] + [chunks] * 8,
        scratch_shapes=[pltpu.VMEM((replicas, d // replicas, 3 * ff), F32)],
        compiler_params=ROOM,
        cost_estimate=pl.CostEstimate(
            flops=12 * n_e * slots * d * ff,
            bytes_accessed=n_e * (12 * d * ff + 4 * slots * d),
            transcendentals=n_e * slots * ff,
        ),
    )(place, order, rows, grads, *weights)
    return out[0], out[1:5], out[5:9]


def returns_kernel(cap, order, me_ref, saved_ref, wg_ref, wu_ref, wd_ref, ret):
    saved = saved_ref[0]
    ff = saved.shape[1] // 3
    hidden, gate_grad, up_grad = saved[:, :ff], saved[:, ff : 2 * ff], saved[:, 2 * ff :]
    out = dot(hidden, wd_ref[0], ((1,), (1,))).astype(BF16)
    entry = dot(gate_grad, wg_ref[0], ((1,), (1,))) + dot(up_grad, wu_ref[0], ((1,), (1,)))
    entry = entry.astype(BF16)
    me, ny = me_ref[0], ret.shape[0] // 2
    for r, (dy, dc) in enumerate(order):
        source = lax.rem(me // 2 + dy, ny) * 2 + lax.rem(me + dc, 2)
        ret[source, 0, 0] = out[r * cap : (r + 1) * cap]
        ret[source, 1, 0] = entry[r * cap : (r + 1) * cap]


def expert_returns(me, order, saved, weights, cap):
    n_e, d, ff = weights[0].shape
    slots = saved.shape[1]
    part = lambda a: pl.BlockSpec((1, *a.shape[1:]), lambda e: (e, 0, 0))
    return pl.pallas_call(
        functools.partial(returns_kernel, cap, order),
        grid=(n_e,),
        in_specs=[SCALARS] + [part(a) for a in (saved, *weights)],
        out_specs=pl.BlockSpec((8, 2, 1, cap, d), lambda e: (0, 0, e, 0, 0)),
        out_shape=jax.ShapeDtypeStruct((8, 2, n_e, cap, d), BF16),
        compiler_params=ROOM,
        cost_estimate=pl.CostEstimate(
            flops=6 * n_e * slots * d * ff,
            bytes_accessed=6 * n_e * (d * ff + slots * ff) + 4 * n_e * slots * d,
            transcendentals=0,
        ),
    )(me, saved, *weights)


def columns(a):
    a = a.astype(F32)
    return jnp.concatenate([a, jnp.zeros((8 - a.shape[0], a.shape[1]), F32)], 0).T


def combine_kernel(cap, ids_ref, gate_ref, _, ret, out_ref, grad_ref):
    n_t, count = ids_ref.shape[1], ret.shape[0] * ret.shape[2]
    eid = lax.broadcasted_iota(jnp.int32, (n_t, count), 1).astype(F32)
    ids = columns(ids_ref[...])
    first, second = ids[:, 0:1] == eid, ids[:, 1:2] == eid
    mask = jnp.where(first | second, 1.0, 0.0).astype(BF16)
    rank = dot(less_than(n_t, True), mask)
    rows = lax.broadcasted_iota(jnp.int32, (count, count * cap), 0)
    cols = lax.broadcasted_iota(jnp.int32, (count, count * cap), 1)
    spread = jnp.where(cols // cap == rows, 1.0, 0.0).astype(BF16)
    slot = (lax.broadcasted_iota(jnp.int32, (n_t, count * cap), 1) % cap).astype(F32)
    hots = [
        jnp.where(dot(jnp.where(m, rank, -1.0).astype(BF16), spread) == slot, 1.0, 0.0)
        for m in (first, second)
    ]
    both = (hots[0] + hots[1]).astype(BF16)
    hots = [h.astype(BF16) for h in hots]
    outs = ret[:, 0].reshape(count * cap, ret.shape[-1])
    grads = ret[:, 1].reshape(count * cap, ret.shape[-1])
    gate = columns(gate_ref[...]) / 65536.0
    total = gate[:, 0:1] * dot(hots[0], outs) + gate[:, 1:2] * dot(hots[1], outs)
    out_ref[...] = total.astype(BF16)
    grad_ref[...] = dot(both, grads).astype(BF16)


def combine(ids, gate, after, ret):
    peers, _, n_e, cap, d = ret.shape
    n_t = ids.shape[1]
    row = jax.ShapeDtypeStruct((n_t, d), BF16)
    return pl.pallas_call(
        functools.partial(combine_kernel, cap),
        grid=(1,),
        in_specs=[whole(ids.shape), whole(gate.shape), pl.BlockSpec(memory_space=pl.ANY), whole(ret.shape)],
        out_specs=[whole(row.shape)] * 2,
        out_shape=[row, row],
        compiler_params=pltpu.CompilerParams(vmem_limit_bytes=24 * 2**20),
        cost_estimate=pl.CostEstimate(
            flops=6 * n_t * d * peers * n_e * cap, bytes_accessed=40 * n_t * d, transcendentals=0
        ),
    )(ids, gate, after, ret)


PLANS = (
    ("xp", "xq", "zp", "zq", "zf"),
    ("xq", "xp", "zq", "zp", "zg"),
    ("zp", "zq", "xp", "xq", "zf"),
    ("zq", "zp", "xq", "xp", "zg"),
)
FAR = {"zf": (3, 6, 5, 0, 7, 2, 1, 4), "zg": (5, 4, 7, 6, 1, 0, 3, 2)}


def partners(kind, nx, nz):
    out = []
    for x in range(nx):
        for z in range(nz):
            at, n = (x, nx) if kind[0] == "x" else (z, nz)
            if kind in FAR:
                at = FAR[kind][at]
            elif kind[1] == "p":
                at = at ^ 1
            else:
                at = (at + 1) % n if at % 2 else (at - 1) % n
            out.append(at * nz + z if kind[0] == "x" else x * nz + at)
    return out


def chunk_orders(nx, nz):
    plans = []
    for plan in PLANS:
        held = [[i] for i in range(nx * nz)]
        for kind in reversed(plan):
            with_ = partners(kind, nx, nz)
            held = [held[with_[i]] + held[i] for i in range(nx * nz)]
        plans.append(held)
    return np.asarray(plans, np.int32).swapaxes(0, 1)


def halve_kernel(n, plans, *refs):
    keep, got, out = refs[:n], refs[n : 2 * n], refs[2 * n :]
    at = 0
    for k_ref, g_ref in zip(keep, got):
        count = k_ref.shape[0] // plans
        half = count // 2
        for v in range(plans):
            for i, ref in enumerate((out[:-1][at // half] if len(out) > 2 else out[0], out[-1])):
                rows = pl.ds(v * count + i * half, half)
                to = 0 if len(out) > 2 and i == 0 else at
                ref[to : to + half] = (k_ref[rows].astype(F32) + g_ref[rows].astype(F32)).astype(BF16)
            at += half


def halve(keep, got, plans=1, apart=False):
    total = sum(a.shape[0] for a in keep) // 2
    shape = lambda count: jax.ShapeDtypeStruct((count, *keep[0].shape[1:]), BF16)
    n = len(keep)
    sends = [shape(total // (n * plans))] * (n * plans) if apart else [shape(total)]
    vmem = pl.BlockSpec(memory_space=pltpu.VMEM)
    out = pl.pallas_call(
        functools.partial(halve_kernel, n, plans),
        in_specs=[vmem] * (2 * n),
        out_specs=[vmem] * (len(sends) + 1),
        out_shape=[*sends, shape(total)],
        compiler_params=pltpu.CompilerParams(vmem_limit_bytes=8 * 2**20),
        cost_estimate=pl.CostEstimate(
            flops=2 * total * keep[0][0].size, bytes_accessed=12 * total * keep[0][0].size, transcendentals=0
        ),
    )(*keep, *got)
    return out[:-1], out[-1]


def halve_plain(keep, got, plans=1, apart=False):
    sends, kept = [], []
    for k, g in zip(keep, got):
        count = k.shape[0] // plans
        half = count // 2
        for v in range(plans):
            a, b, c = v * count, v * count + half, (v + 1) * count
            sends.append((k[a:b].astype(F32) + g[a:b].astype(F32)).astype(BF16))
            kept.append((k[b:c].astype(F32) + g[b:c].astype(F32)).astype(BF16))
    join = lambda a: a[0] if len(a) == 1 else jnp.concatenate(a, 0)
    return (sends if apart else [join(sends)]), join(kept)


def reduce_grads(send, keep, nx, nz):
    swap = lambda a, kind: lax.ppermute(a, "dp", list(enumerate(partners(kind, nx, nz))))
    got = [swap(send[v], PLANS[v][0]) for v in range(4)]
    held = [halve_plain([keep[v]], [got[v]]) for v in range(4)]
    for step in (1, 2):
        got = [swap(held[v][0][0], PLANS[v][step]) for v in range(4)]
        held = [halve([held[v][1]], [got[v]]) for v in range(4)]
    got = [swap(held[v][0][0], PLANS[v][3]) for v in range(4)]
    terms, sends = [], []
    for a, b in ((0, 2), (1, 3)):
        sent, kept = halve([held[a][1], held[b][1]], [got[a], got[b]])
        terms.append((kept, [swap(sent[0], PLANS[a][4])]))
        sends += sent
    return [k for k, _ in terms], [g for _, g in terms], sends


def shards(nx, nz, tokens, expert_ids, gate_fixed, cotangent, w_gate, w_up, w_down):
    n_t, top = expert_ids.shape
    n_e, d, ff = w_gate.shape
    peers = lax.axis_size("expert")
    ny = peers // 2
    replicas = nx * nz
    cap = n_t * top * 2 // (n_e * peers)
    scale = float(n_t * replicas * top // n_e) ** (-0.5)
    me = lax.axis_index("expert")
    place = lax.axis_index("dp")

    def to(a, dy, dc):
        perm = [(y * 2 + c, ((y + dy) % ny) * 2 + (c ^ dc)) for y in range(ny) for c in range(2)]
        return lax.ppermute(a, "expert", perm)

    ids, gate = expert_ids.T, gate_fixed.T
    tok = {(0, 0): with_meta(ids, gate, tokens)}
    cot = {(0, 0): cotangent}
    cot[3, 0], cot[1, 0] = to(cotangent, 1, 0), to(cotangent, -1, 0)
    tok[0, 1], cot[0, 1] = to(tok[0, 0], 0, 1), to(cotangent, 0, 1)
    later, cot[3, 0], cot[1, 0], tok[0, 1], cot[0, 1] = lax.optimization_barrier(
        (tok[0, 0], cot[3, 0], cot[1, 0], tok[0, 1], cot[0, 1])
    )
    tok[3, 0], tok[1, 0] = to(later, 1, 0), to(later, -1, 0)
    cot[3, 1], cot[1, 1] = to(cot[3, 0], 0, 1), to(cot[1, 0], 0, 1)
    cot[2, 0], tok[2, 0] = to(cot[3, 0], 1, 0), to(tok[1, 0], -1, 0)
    tok[3, 1], tok[1, 1] = to(tok[3, 0], 0, 1), to(tok[1, 0], 0, 1)
    order = tuple((dy, dc) for dy in (0, 1, 3, 2) for dc in range(2))
    mine, here = me.reshape(1), place.reshape(1)
    near = pack(mine, [tok[r] for r in order[:6]], [cot[r] for r in order[:6]], cap, n_e)
    tok[2, 1], cot[2, 1] = to(tok[2, 0], 0, 1), to(cot[2, 0], 0, 1)
    rows, grads = pack(mine, [tok[r] for r in order[6:]], [cot[r] for r in order[6:]], cap, n_e, near)
    chunks = jnp.asarray(chunk_orders(nx, nz).reshape(replicas, -1))
    weights = (w_gate, w_up, w_down)
    saved, send, keep = expert_grads(here, chunks, rows, grads, weights, scale)
    keep, got, last = reduce_grads(send, keep, nx, nz)
    ret = expert_returns(mine, order, saved, weights, cap)
    back = lax.all_to_all(ret, "expert", split_axis=0, concat_axis=0, tiled=True)
    layer_out, input_grad = combine(ids, gate, last[-1], back)
    got, layer_out = lax.optimization_barrier((got, layer_out))
    total = [k.astype(F32) + jnp.concatenate(g, 0).astype(F32) for k, g in zip(keep, got)]
    total = jnp.concatenate([t[i : i + 1] for i in range(2) for t in total], 0)
    return (layer_out, input_grad, total[:, :, :ff], total[:, :, ff : 2 * ff], total[:, :, 2 * ff :])


def solution(mesh):
    nx = 4
    nz = mesh.shape["dp"] // nx
    return jax.shard_map(
        functools.partial(shards, nx, nz),
        mesh=mesh,
        in_specs=(P(("dp", "expert"), None),) * 4 + (P("expert", None, None),) * 3,
        out_specs=(P(("dp", "expert"), None),) * 2 + (P("expert", "dp", None),) * 3,
        check_vma=False,
    )
```

```python
import functools

import jax
import jax.numpy as jnp
import numpy as np
from jax import lax
from jax.experimental import pallas as pl
from jax.experimental.pallas import tpu as pltpu
from jax.sharding import PartitionSpec as P

F32, BF16 = jnp.float32, jnp.bfloat16
META = 16


def dot(a, b, dims=((1,), (0,))):
    return lax.dot_general(a, b, (dims, ((), ())), preferred_element_type=F32)


ROOM = pltpu.CompilerParams(vmem_limit_bytes=61 * 2**20)
SCALARS = pl.BlockSpec(memory_space=pltpu.SMEM)


def whole(shape):
    return pl.BlockSpec(shape, lambda i: (0,) * len(shape))


def less_than(size, transposed):
    rows = lax.broadcasted_iota(jnp.int32, (size, size), 0)
    cols = lax.broadcasted_iota(jnp.int32, (size, size), 1)
    return ((cols < rows) if transposed else (rows < cols)).astype(F32).astype(BF16)


def meta_kernel(ids_ref, gate_ref, tok_ref, out_ref):
    n_t, d = tok_ref.shape
    ids, gate = ids_ref[...], gate_ref[...]
    high, low = gate // 256, gate % 256
    meta = jnp.concatenate([ids, high, low], 0).astype(F32)
    meta = jnp.concatenate([meta, jnp.zeros((META - 6, n_t), F32)], 0)
    out_ref[:n_t, :] = tok_ref[...]
    out_ref[n_t:, :n_t] = meta.astype(BF16)
    out_ref[n_t:, n_t:] = jnp.zeros((META, d - n_t), BF16)


def with_meta(ids, gate, tokens):
    n_t, d = tokens.shape
    return pl.pallas_call(
        meta_kernel,
        grid=(1,),
        in_specs=[whole(ids.shape), whole(gate.shape), whole(tokens.shape)],
        out_specs=whole((n_t + META, d)),
        out_shape=jax.ShapeDtypeStruct((n_t + META, d), BF16),
        compiler_params=ROOM,
        cost_estimate=pl.CostEstimate(flops=n_t * d, bytes_accessed=4 * n_t * d, transcendentals=0),
    )(ids, gate, tokens)


def pack_kernel(n, cap, n_e, me_ref, *refs):
    tok, cot = refs[:n], refs[n : 2 * n]
    rows_ref, grads_ref = refs[-2:]
    n_t = cot[0].shape[0]
    eid = (me_ref[0] * n_e + lax.broadcasted_iota(jnp.int32, (n_e, n_t), 0)).astype(F32)
    masks, gates = [], []
    for r in range(n):
        meta = tok[r][n_t : n_t + META, :n_t].astype(F32)
        row = lambda i: jnp.broadcast_to(meta[i : i + 1], (n_e, n_t))
        first, second = row(0) == eid, row(1) == eid
        g0 = (row(2) * 256.0 + row(4)) / 65536.0
        g1 = (row(3) * 256.0 + row(5)) / 65536.0
        masks.append(jnp.where(first | second, 1.0, 0.0))
        gates.append(jnp.where(first, g0, jnp.where(second, g1, 0.0)))
    mask = jnp.concatenate(masks, 0)
    rank = jnp.where(mask > 0.5, dot(mask.astype(BF16), less_than(n_t, False)), -1.0)
    slot = lax.broadcasted_iota(jnp.int32, (cap, n_t), 0).astype(F32)
    for r in range(n):
        hots, slot_gates = [], []
        for e in range(n_e):
            i = r * n_e + e
            hot = jnp.where(jnp.broadcast_to(rank[i : i + 1], (cap, n_t)) == slot, 1.0, 0.0)
            hots.append(hot)
            slot_gates.append(jnp.sum(hot * gates[r][e : e + 1], axis=1, keepdims=True))
        hot = jnp.concatenate(hots, 0).astype(BF16)
        slot_gate = jnp.concatenate(slot_gates, 0)
        rows = dot(hot, tok[r][:n_t, :]).astype(BF16)
        grads = (slot_gate * dot(hot, cot[r][...])).astype(BF16)
        for e in range(n_e):
            rows_ref[e, r * cap : (r + 1) * cap, :] = rows[e * cap : (e + 1) * cap]
            grads_ref[e, r * cap : (r + 1) * cap, :] = grads[e * cap : (e + 1) * cap]


def pack(me, tok, cot, cap, n_e, before=()):
    n, (n_t, d) = len(cot), cot[0].shape
    out = jax.ShapeDtypeStruct((n_e, 8 * cap, d), BF16)
    at = 8 // n - 1 if before else 0
    return pl.pallas_call(
        functools.partial(pack_kernel, n, cap, n_e),
        grid=(1,),
        in_specs=[SCALARS]
        + [whole(a.shape) for a in (*tok, *cot)]
        + [pl.BlockSpec(memory_space=pl.ANY)] * len(before),
        out_specs=[pl.BlockSpec((n_e, n * cap, d), lambda i: (0, at, 0))] * 2,
        out_shape=[out, out],
        input_output_aliases={2 * n + 1 + i: i for i in range(len(before))},
        compiler_params=ROOM,
        cost_estimate=pl.CostEstimate(
            flops=4 * n * n_e * cap * n_t * d, bytes_accessed=4 * n * (n_t + n_e * cap) * d, transcendentals=0
        ),
    )(me, *tok, *cot, *before)


def grads_kernel(scale, place_ref, order_ref, x_ref, dy_ref, wg_ref, wu_ref, wd_ref, *refs):
    n_e = pl.num_programs(0)
    saved, send, keep, acc = refs[0], refs[1:5], refs[5:9], refs[9]
    step = pl.program_id(0)
    x, dy = x_ref[0], dy_ref[0]
    pre_gate, pre_up = dot(x, wg_ref[0]), dot(x, wu_ref[0])
    hidden_grad = dot(dy, wd_ref[0])
    sig = jax.nn.sigmoid(pre_gate)
    act = pre_gate * sig
    hidden = (act * pre_up).astype(BF16)
    gate_grad = (hidden_grad * pre_up * sig * (1.0 + pre_gate * (1.0 - sig))).astype(BF16)
    up_grad = (hidden_grad * act).astype(BF16)
    ff, replicas = hidden.shape[1], acc.shape[0]
    half = replicas // 2
    both = jnp.concatenate([gate_grad, up_grad], 1)
    saved[0, :, :ff] = hidden
    saved[0, :, ff:] = both
    acc[:, :, : 2 * ff] = (dot(x, both, ((0,), (0,))) * scale).reshape(replicas, -1, 2 * ff)
    acc[:, :, 2 * ff :] = (dot(dy, hidden, ((0,), (0,))) * scale).reshape(replicas, -1, ff)
    for i in range(4):

        @pl.when(step == i)
        def _(i=i):
            for p in range(replicas):
                chunk = order_ref[place_ref[0], i * replicas + p]
                (send if p < half else keep)[i][p % half] = acc[chunk].astype(BF16)


def expert_grads(place, order, rows, grads, weights, scale):
    n_e, d, ff = weights[0].shape
    replicas = order.shape[0]
    slots = rows.shape[1]
    part = lambda a: pl.BlockSpec((1, *a.shape[1:]), lambda e: (e, 0, 0))
    saved = jax.ShapeDtypeStruct((n_e, slots, 3 * ff), BF16)
    chunks = jax.ShapeDtypeStruct((replicas // 2, d // replicas, 3 * ff), BF16)
    out = pl.pallas_call(
        functools.partial(grads_kernel, scale),
        grid=(n_e,),
        in_specs=[SCALARS] * 2 + [part(a) for a in (rows, grads, *weights)],
        out_specs=[part(saved)] + [whole(chunks.shape)] * 8,
        out_shape=[saved] + [chunks] * 8,
        scratch_shapes=[pltpu.VMEM((replicas, d // replicas, 3 * ff), F32)],
        compiler_params=ROOM,
        cost_estimate=pl.CostEstimate(
            flops=12 * n_e * slots * d * ff,
            bytes_accessed=n_e * (12 * d * ff + 4 * slots * d),
            transcendentals=n_e * slots * ff,
        ),
    )(place, order, rows, grads, *weights)
    return out[0], out[1:5], out[5:9]


def returns_kernel(cap, order, me_ref, saved_ref, wg_ref, wu_ref, wd_ref, ret):
    saved = saved_ref[0]
    ff = saved.shape[1] // 3
    hidden, gate_grad, up_grad = saved[:, :ff], saved[:, ff : 2 * ff], saved[:, 2 * ff :]
    out = dot(hidden, wd_ref[0], ((1,), (1,))).astype(BF16)
    entry = dot(gate_grad, wg_ref[0], ((1,), (1,))) + dot(up_grad, wu_ref[0], ((1,), (1,)))
    entry = entry.astype(BF16)
    me, ny = me_ref[0], ret.shape[0] // 2
    for r, (dy, dc) in enumerate(order):
        source = lax.rem(me // 2 + dy, ny) * 2 + lax.rem(me + dc, 2)
        ret[source, 0, 0] = out[r * cap : (r + 1) * cap]
        ret[source, 1, 0] = entry[r * cap : (r + 1) * cap]


def expert_returns(me, order, saved, weights, cap):
    n_e, d, ff = weights[0].shape
    slots = saved.shape[1]
    part = lambda a: pl.BlockSpec((1, *a.shape[1:]), lambda e: (e, 0, 0))
    return pl.pallas_call(
        functools.partial(returns_kernel, cap, order),
        grid=(n_e,),
        in_specs=[SCALARS] + [part(a) for a in (saved, *weights)],
        out_specs=pl.BlockSpec((8, 2, 1, cap, d), lambda e: (0, 0, e, 0, 0)),
        out_shape=jax.ShapeDtypeStruct((8, 2, n_e, cap, d), BF16),
        compiler_params=ROOM,
        cost_estimate=pl.CostEstimate(
            flops=6 * n_e * slots * d * ff,
            bytes_accessed=6 * n_e * (d * ff + slots * ff) + 4 * n_e * slots * d,
            transcendentals=0,
        ),
    )(me, saved, *weights)


def columns(a):
    a = a.astype(F32)
    return jnp.concatenate([a, jnp.zeros((8 - a.shape[0], a.shape[1]), F32)], 0).T


def combine_kernel(cap, ids_ref, gate_ref, _, ret, out_ref, grad_ref):
    n_t, count = ids_ref.shape[1], ret.shape[0] * ret.shape[2]
    eid = lax.broadcasted_iota(jnp.int32, (n_t, count), 1).astype(F32)
    ids = columns(ids_ref[...])
    first, second = ids[:, 0:1] == eid, ids[:, 1:2] == eid
    mask = jnp.where(first | second, 1.0, 0.0).astype(BF16)
    rank = dot(less_than(n_t, True), mask)
    rows = lax.broadcasted_iota(jnp.int32, (count, count * cap), 0)
    cols = lax.broadcasted_iota(jnp.int32, (count, count * cap), 1)
    spread = jnp.where(cols // cap == rows, 1.0, 0.0).astype(BF16)
    slot = (lax.broadcasted_iota(jnp.int32, (n_t, count * cap), 1) % cap).astype(F32)
    hots = [
        jnp.where(dot(jnp.where(m, rank, -1.0).astype(BF16), spread) == slot, 1.0, 0.0)
        for m in (first, second)
    ]
    both = (hots[0] + hots[1]).astype(BF16)
    hots = [h.astype(BF16) for h in hots]
    outs = ret[:, 0].reshape(count * cap, ret.shape[-1])
    grads = ret[:, 1].reshape(count * cap, ret.shape[-1])
    gate = columns(gate_ref[...]) / 65536.0
    total = gate[:, 0:1] * dot(hots[0], outs) + gate[:, 1:2] * dot(hots[1], outs)
    out_ref[...] = total.astype(BF16)
    grad_ref[...] = dot(both, grads).astype(BF16)


def combine(ids, gate, after, ret):
    peers, _, n_e, cap, d = ret.shape
    n_t = ids.shape[1]
    row = jax.ShapeDtypeStruct((n_t, d), BF16)
    return pl.pallas_call(
        functools.partial(combine_kernel, cap),
        grid=(1,),
        in_specs=[whole(ids.shape), whole(gate.shape), pl.BlockSpec(memory_space=pl.ANY), whole(ret.shape)],
        out_specs=[whole(row.shape)] * 2,
        out_shape=[row, row],
        compiler_params=pltpu.CompilerParams(vmem_limit_bytes=24 * 2**20),
        cost_estimate=pl.CostEstimate(
            flops=6 * n_t * d * peers * n_e * cap, bytes_accessed=40 * n_t * d, transcendentals=0
        ),
    )(ids, gate, after, ret)


PLANS = (
    ("xp", "xq", "zp", "zq", "zf"),
    ("xq", "xp", "zq", "zp", "zg"),
    ("zp", "zq", "xp", "xq", "zf"),
    ("zq", "zp", "xq", "xp", "zg"),
)
FAR = {"zf": (3, 6, 5, 0, 7, 2, 1, 4), "zg": (5, 4, 7, 6, 1, 0, 3, 2)}


def partners(kind, nx, nz):
    out = []
    for x in range(nx):
        for z in range(nz):
            at, n = (x, nx) if kind[0] == "x" else (z, nz)
            if kind in FAR:
                at = FAR[kind][at]
            elif kind[1] == "p":
                at = at ^ 1
            else:
                at = (at + 1) % n if at % 2 else (at - 1) % n
            out.append(at * nz + z if kind[0] == "x" else x * nz + at)
    return out


def chunk_orders(nx, nz):
    plans = []
    for plan in PLANS:
        held = [[i] for i in range(nx * nz)]
        for kind in reversed(plan):
            with_ = partners(kind, nx, nz)
            held = [held[with_[i]] + held[i] for i in range(nx * nz)]
        plans.append(held)
    return np.asarray(plans, np.int32).swapaxes(0, 1)


def halve_kernel(n, plans, *refs):
    keep, got, out = refs[:n], refs[n : 2 * n], refs[2 * n :]
    at = 0
    for k_ref, g_ref in zip(keep, got):
        count = k_ref.shape[0] // plans
        half = count // 2
        for v in range(plans):
            for i, ref in enumerate((out[:-1][at // half] if len(out) > 2 else out[0], out[-1])):
                rows = pl.ds(v * count + i * half, half)
                to = 0 if len(out) > 2 and i == 0 else at
                ref[to : to + half] = (k_ref[rows].astype(F32) + g_ref[rows].astype(F32)).astype(BF16)
            at += half


def halve(keep, got, plans=1, apart=False):
    total = sum(a.shape[0] for a in keep) // 2
    shape = lambda count: jax.ShapeDtypeStruct((count, *keep[0].shape[1:]), BF16)
    n = len(keep)
    sends = [shape(total // (n * plans))] * (n * plans) if apart else [shape(total)]
    vmem = pl.BlockSpec(memory_space=pltpu.VMEM)
    out = pl.pallas_call(
        functools.partial(halve_kernel, n, plans),
        in_specs=[vmem] * (2 * n),
        out_specs=[vmem] * (len(sends) + 1),
        out_shape=[*sends, shape(total)],
        compiler_params=pltpu.CompilerParams(vmem_limit_bytes=8 * 2**20),
        cost_estimate=pl.CostEstimate(
            flops=2 * total * keep[0][0].size, bytes_accessed=12 * total * keep[0][0].size, transcendentals=0
        ),
    )(*keep, *got)
    return out[:-1], out[-1]


def halve_plain(keep, got, plans=1, apart=False):
    sends, kept = [], []
    for k, g in zip(keep, got):
        count = k.shape[0] // plans
        half = count // 2
        for v in range(plans):
            a, b, c = v * count, v * count + half, (v + 1) * count
            sends.append((k[a:b].astype(F32) + g[a:b].astype(F32)).astype(BF16))
            kept.append((k[b:c].astype(F32) + g[b:c].astype(F32)).astype(BF16))
    join = lambda a: a[0] if len(a) == 1 else jnp.concatenate(a, 0)
    return (sends if apart else [join(sends)]), join(kept)


def reduce_grads(send, keep, nx, nz):
    swap = lambda a, kind: lax.ppermute(a, "dp", list(enumerate(partners(kind, nx, nz))))
    got = [swap(send[v], PLANS[v][0]) for v in range(4)]
    held = [(halve_plain if v < 4 else halve)([keep[v]], [got[v]]) for v in range(4)]
    for step in (1, 2):
        got = [swap(held[v][0][0], PLANS[v][step]) for v in range(4)]
        held = [halve([held[v][1]], [got[v]]) for v in range(4)]
    got = [swap(held[v][0][0], PLANS[v][3]) for v in range(4)]
    terms, sends = [], []
    for a, b in ((0, 2), (1, 3)):
        sent, kept = halve([held[a][1], held[b][1]], [got[a], got[b]])
        terms.append((kept, [swap(sent[0], PLANS[a][4])]))
        sends += sent
    return [k for k, _ in terms], [g for _, g in terms], sends


def finish_kernel(a_ref, b_ref, c_ref, d_ref, *outs):
    ff = outs[0].shape[-1]
    for i in range(a_ref.shape[0]):
        for j, (k, g) in enumerate(((a_ref, c_ref), (b_ref, d_ref))):
            total = k[i].astype(F32) + g[i].astype(F32)
            for n, out in enumerate(outs):
                out[2 * i + j] = total[:, n * ff : (n + 1) * ff]


def finish(keep, got):
    pairs, own, wide = keep[0].shape
    out = jax.ShapeDtypeStruct((2 * pairs, own, wide // 3), F32)
    return pl.pallas_call(
        finish_kernel,
        grid=(1,),
        in_specs=[whole(keep[0].shape)] * 4,
        out_specs=[whole(out.shape)] * 3,
        out_shape=[out] * 3,
        cost_estimate=pl.CostEstimate(flops=2 * out.size, bytes_accessed=24 * out.size, transcendentals=0),
    )(*keep, *got)


def shards(nx, nz, tokens, expert_ids, gate_fixed, cotangent, w_gate, w_up, w_down):
    n_t, top = expert_ids.shape
    n_e, d, ff = w_gate.shape
    peers = lax.axis_size("expert")
    ny = peers // 2
    replicas = nx * nz
    cap = n_t * top * 2 // (n_e * peers)
    scale = float(n_t * replicas * top // n_e) ** (-0.5)
    me = lax.axis_index("expert")
    place = lax.axis_index("dp")

    def to(a, dy, dc):
        perm = [(y * 2 + c, ((y + dy) % ny) * 2 + (c ^ dc)) for y in range(ny) for c in range(2)]
        return lax.ppermute(a, "expert", perm)

    ids, gate = expert_ids.T, gate_fixed.T
    tok = {(0, 0): with_meta(ids, gate, tokens)}
    cot = {(0, 0): cotangent}
    cot[3, 0], cot[1, 0] = to(cotangent, 1, 0), to(cotangent, -1, 0)
    tok[0, 1], cot[0, 1] = to(tok[0, 0], 0, 1), to(cotangent, 0, 1)
    own, cot[3, 0], cot[1, 0] = lax.optimization_barrier((tok[0, 0], cot[3, 0], cot[1, 0]))
    tok[3, 0], tok[1, 0] = to(own, 1, 0), to(own, -1, 0)
    cot[3, 1], cot[1, 1] = to(cot[3, 0], 0, 1), to(cot[1, 0], 0, 1)
    by_c, tok[3, 0], tok[1, 0] = lax.optimization_barrier((cot[3, 0], tok[3, 0], tok[1, 0]))
    cot[2, 0], tok[2, 0] = to(by_c, 1, 0), to(tok[1, 0], -1, 0)
    tok[3, 1], tok[1, 1] = to(tok[3, 0], 0, 1), to(tok[1, 0], 0, 1)
    order = tuple((dy, dc) for dy in (0, 1, 3, 2) for dc in range(2))
    mine, here = me.reshape(1), place.reshape(1)
    near = pack(mine, [tok[r] for r in order[:6]], [cot[r] for r in order[:6]], cap, n_e)
    near, tok[2, 0], cot[2, 0] = lax.optimization_barrier((near, tok[2, 0], cot[2, 0]))
    tok[2, 1], cot[2, 1] = to(tok[2, 0], 0, 1), to(cot[2, 0], 0, 1)
    rows, grads = pack(mine, [tok[r] for r in order[6:]], [cot[r] for r in order[6:]], cap, n_e, near)
    chunks = jnp.asarray(chunk_orders(nx, nz).reshape(replicas, -1))
    weights = (w_gate, w_up, w_down)
    saved, send, keep = expert_grads(here, chunks, rows, grads, weights, scale)
    keep, got, last = reduce_grads(send, keep, nx, nz)
    ret = expert_returns(mine, order, saved, weights, cap)
    back = lax.all_to_all(ret, "expert", split_axis=0, concat_axis=0, tiled=True)
    layer_out, input_grad = combine(ids, gate, last[-1], back)
    got, layer_out = lax.optimization_barrier((got, layer_out))
    return (layer_out, input_grad, *finish(keep, [g[0] for g in got]))


def solution(mesh):
    nx = 4
    nz = mesh.shape["dp"] // nx
    return jax.shard_map(
        functools.partial(shards, nx, nz),
        mesh=mesh,
        in_specs=(P(("dp", "expert"), None),) * 4 + (P("expert", None, None),) * 3,
        out_specs=(P(("dp", "expert"), None),) * 2 + (P("expert", "dp", None),) * 3,
        check_vma=False,
    )
```
